256 devices in a mesh: row: 16 (over y, z_hi), col: 16 (over x, z_lo, core).
Axes of the slice: x: 4, y: 4, z: 8 (z_hi: 4, z_lo: 2; z = z_hi * 2 + z_lo), core: 2. Of those that a mesh axis runs over, the one named last changes fastest.
Arguments:
- tokens: bfloat16 [4096, 3072], P('row', 'col'), may hold values from -6 to 6
- out_grad: bfloat16 [4096, 3072], P('row', 'col'), may hold values from -12 to 12
- w_up: bfloat16 [3072, 12288], P('row', 'col'), may hold values from -0.109375 to 0.109375
- w_down: bfloat16 [3072, 12288], P('row', 'col'), may hold values from -0.109375 to 0.109375
Outputs:
- input_grad: bfloat16 [4096, 3072], P('row', 'col')
- up_grad: float32 [3072, 12288], P('row', 'col')
- down_grad: float32 [3072, 12288], P('row', 'col')
The draws below stay inside these ranges and needn't reach their ends.
All inputs are finite; a program needn't handle non-finite values.
Results may differ from the reference program's by a relative error of at most 0.0049.
Values may be sent and summed in bfloat16 or wider, within the bound.
A program may use at most 128 MiB of HBM per device.

```python
import math
import jax
import jax.numpy as jnp

D = 3072
FF = 12288
TOK_ROW = 256
TOKENS = 4096
N_ROW = 16


def levels(own_key, extent, cuts, smallest, top_value):
    gain = 1.0
    for dim, blocks in cuts:
        steps = jax.random.uniform(jax.random.fold_in(jax.random.fold_in(own_key, 6), dim), (blocks,), jnp.float32, smallest / len(cuts), top_value / len(cuts))
        gain = gain * jnp.repeat(jnp.exp(steps), extent[dim] // blocks).reshape((-1,) + (1,) * (len(extent) - 1 - dim))
    return gain


def noise(key, extent, deviation, most, shards=(), dtype=jnp.bfloat16):
    values = jax.random.normal(key, extent, jnp.float32) * deviation
    if len(shards) > 0:
        values = levels(key, extent, shards, -0.22, 0.18) * values
    return jnp.clip(values, min=-most, max=most).astype(dtype)


def setup_inputs(seed: int = 0) -> dict:
    streams_of = jax.random.split(jax.random.key(seed), 5)
    tokens = noise(streams_of[0], (TOKENS, D), 1.0, 6.0, ((0, 16), (1, 16)))
    out_grad = noise(streams_of[1], (TOKENS, D), 2.0, 12.0, ((0, 16), (1, 16)))
    w_up = noise(streams_of[2], (D, FF), D ** -0.5, 0.109375, ((0, 16), (1, 16)))
    w_down = noise(streams_of[3], (D, FF), D ** -0.5, 0.109375, ((0, 16), (1, 16)))
    return {"tokens": tokens, "out_grad": out_grad, "w_up": w_up, "w_down": w_down}


gelu_coef = math.sqrt(2.0 / math.pi)
cubic_coef = 0.044715

def gelu_pair(hidden):
    inner = gelu_coef * (hidden + cubic_coef * hidden * hidden * hidden)
    tangent = jnp.tanh(inner)
    active = 0.5 * hidden * (1.0 + tangent)
    slope = 0.5 * (1.0 + tangent) + 0.5 * hidden * (1.0 - tangent * tangent) * gelu_coef * (1.0 + 3.0 * cubic_coef * hidden * hidden)
    return (active, slope)

def token_sum(left, right):
    factor = 1.0 / math.sqrt(N_ROW * TOK_ROW)
    return jnp.dot(left.T, right, preferred_element_type=jnp.float32) * factor

def reference(tokens, out_grad, w_up, w_down):
    hidden = jnp.dot(tokens, w_up, preferred_element_type=jnp.float32)
    active, slope = gelu_pair(hidden)
    active = active.astype(jnp.bfloat16)
    active_grad = jnp.dot(out_grad, w_down, preferred_element_type=jnp.float32)
    hidden_grad = (active_grad * slope).astype(jnp.bfloat16)
    input_grad = jnp.dot(hidden_grad, w_up.T, preferred_element_type=jnp.float32).astype(jnp.bfloat16)
    up_grad = token_sum(tokens, hidden_grad)
    down_grad = token_sum(out_grad, active)
    return (input_grad, up_grad, down_grad)
```

```python
import math

import jax
import jax.numpy as jnp
from jax import lax
from jax.experimental import pallas as pl
from jax.experimental.pallas import tpu as pltpu
from jax.sharding import PartitionSpec as P

gelu_coef = math.sqrt(2.0 / math.pi)
cubic_coef = 0.044715
MESH = pl.DeviceIdType.MESH
BF16 = jnp.bfloat16
F32 = jnp.float32


def gelu_pair(hidden):
    inner = gelu_coef * (hidden + cubic_coef * hidden * hidden * hidden)
    tangent = jnp.tanh(inner)
    active = 0.5 * hidden * (1.0 + tangent)
    slope = 0.5 * (1.0 + tangent) + 0.5 * hidden * (1.0 - tangent * tangent) * gelu_coef * (
        1.0 + 3.0 * cubic_coef * hidden * hidden
    )
    return (active, slope)


class Slots:
    def __init__(self):
        self.at = {}
        self.count = 0

    def __call__(self, key, extent=1):
        if key not in self.at:
            self.at[key] = self.count
            self.count += extent
        return self.at[key]


SEMS = 256


def kernel(
    tok, og, wu, wd, dw_out, ig_out,
    X, W, H, hb, igs, igr, zs, zr, own_sum, last, ds, dr, dws, dwr, dwl,
    send_sems, recv_sems, local_sems,
):
    row, col = lax.axis_index("row"), lax.axis_index("col")
    x, y = lax.div(col, 4), lax.div(row, 4)
    zh, zl, k = lax.rem(row, 4), lax.rem(lax.div(col, 2), 2), lax.rem(col, 2)
    z = 2 * zh + zl
    o = 1 - k
    mod4 = lambda v: lax.rem(v + 8, 4)
    mod8 = lambda v: lax.rem(v + 16, 8)

    def dev(dx=0, dy=0, zz=None, core=None):
        zz = z if zz is None else zz
        core = k if core is None else core
        xx = mod4(x + dx) if dx else x
        yy = mod4(y + dy) if dy else y
        return (yy * 4 + lax.div(zz, 2), xx * 4 + lax.rem(zz, 2) * 2 + core)

    sib = dev(core=o)
    xp, xm = dev(dx=1), dev(dx=-1)
    yp, ym = dev(dy=1), dev(dy=-1)
    zp, zm = dev(zz=mod8(z + 1)), dev(zz=mod8(z - 1))

    barrier = pltpu.get_barrier_semaphore()
    partners = [sib, xp, xm, yp, ym]
    for rel in range(1, 8):
        for core in (k, o):
            partners.append(dev(zz=mod8(z + rel), core=core))
    for partner in partners:
        pl.semaphore_signal(barrier, inc=1, device_id=partner, device_id_type=MESH)
    pl.semaphore_wait(barrier, len(partners))

    send_no, recv_no, local_no = Slots(), Slots(), Slots()
    sent = []

    def copy_to(src, dst, key, device, recv_at=None):
        recv_at = recv_no(key) if recv_at is None else recv_at
        return pltpu.make_async_remote_copy(
            src_ref=src,
            dst_ref=dst,
            send_sem=send_sems.at[send_no(key)],
            recv_sem=recv_sems.at[recv_at],
            device_id=device,
            device_id_type=MESH,
        )

    def send(src, dst, key, device, recv_at=None):
        copy = copy_to(src, dst, key, device, recv_at)
        copy.start()
        sent.append((None, copy))

    def send_unless(own, src, dst, key, device, recv_at):
        copy = copy_to(src, dst, key, device, recv_at)
        local = pltpu.make_async_copy(src, dst, recv_sems.at[recv_at])

        @pl.when(own)
        def _():
            local.start()

        @pl.when(jnp.logical_not(own))
        def _():
            copy.start()

        sent.append((jnp.logical_not(own), copy))

    def recv(dst, key=None, at=None):
        at = recv_no(key) if at is None else at
        pltpu.make_async_remote_copy(
            src_ref=dst,
            dst_ref=dst,
            send_sem=send_sems.at[0],
            recv_sem=recv_sems.at[at],
            device_id=sib,
            device_id_type=MESH,
        ).wait_recv()

    def w_rows(a, yy, zz):
        return W.at[a, yy, pl.ds(pl.multiple_of(zz * 192, 192), 192), :]

    w_base = recv_no("w", 4)
    for h in range(2):
        for a, src in enumerate((wu, wd)):
            zt = 2 * k + h
            send_unless(
                jnp.logical_and(zt == zh, k == a),
                src.at[:, h * 384 : (h + 1) * 384],
                w_rows(a, y, zh),
                ("w", h, a),
                dev(zz=2 * zt + zl, core=a),
                w_base + zh,
            )

    def shard(a, xx, zz):
        return X.at[
            a, xx,
            pl.ds(pl.multiple_of(lax.rem(zz, 2) * 384, 384), 384),
            pl.ds(pl.multiple_of(lax.div(zz, 2) * 128, 128), 128),
        ]

    def part(a, core):
        return X.at[
            a, x,
            pl.ds(pl.multiple_of(zl * 384 + core * 192, 192), 192),
            pl.ds(pl.multiple_of(zh * 128, 128), 128),
        ]

    mine = pl.ds(pl.multiple_of(k * 128, 128), 128)
    other = pl.ds(pl.multiple_of(o * 128, 128), 128)
    locals_ = []
    for a, src in enumerate((tok, og)):
        send(src.at[:, other], part(a, k), ("half", a), sib)
        copy = pltpu.make_async_copy(src.at[:, mine], part(a, k), local_sems.at[a])
        copy.start()
        locals_.append(copy)
    for a in range(2):
        locals_[a].wait()
        recv(part(a, o), ("half", a))

    steps = [[(0, 0)], [(-1, 1), (1, -1)], [(-2, 1), (2, -1)], [(-3, 1), (3, -1)], [(4, 0)]]

    def arrive(step):
        for a in range(2):
            for rel, way in steps[step]:
                block = shard(a, x, mod8(z + rel))
                if step == 0:
                    send(block, block, ("z", -1, a), zp)
                    send(block, block, ("z", 1, a), zm)
                else:
                    recv(block, ("z", rel, a))
                    if way == 1 and (step < 3 or (step == 3 and a == 0)):
                        send(block, block, ("z", rel - 1 if step < 3 else 4, a), zp)
                    if way == -1 and (step < 3 or (step == 3 and a == 1)):
                        send(block, block, ("z", rel + 1 if step < 3 else 4, a), zm)
                send(block, block, ("x", -1, rel, a), xp)
                send(block, block, ("x", 1, rel, a), xm)

    def across(step):
        for a in range(2):
            for rel, _ in steps[step]:
                zz = mod8(z + rel)
                left, right = shard(a, mod4(x - 1), zz), shard(a, mod4(x + 1), zz)
                recv(left, ("x", -1, rel, a))
                if a == 0:
                    send(left, left, ("x", 2, rel, a), xp)
                recv(right, ("x", 1, rel, a))
                if a == 1:
                    send(right, right, ("x", 2, rel, a), xm)

    order = [0, 1, 3, 2]
    arrive(0)

    for i, off in enumerate(order):
        zz = mod4(zh + off)
        block = w_rows(k, y, zz)
        recv(block, at=w_base + zz)
        send(block, block, ("wy", -1, i), yp)
        send(block, block, ("wy", 1, i), ym)
        send(block, block, ("wk", 0, i), sib)
        if i == 1:
            arrive(1)
    for i, off in enumerate(order):
        zz = mod4(zh + off)
        left, right = w_rows(k, mod4(y - 1), zz), w_rows(k, mod4(y + 1), zz)
        recv(left, ("wy", -1, i))
        if i < 2:
            send(left, left, ("wy", 2, i), yp)
        send(left, left, ("wk", -1, i), sib)
        recv(right, ("wy", 1, i))
        if i >= 2:
            send(right, right, ("wy", 2, i), ym)
        send(right, right, ("wk", 1, i), sib)
        if i == 0:
            across(0)
            arrive(2)
        if i == 2:
            across(1)
            arrive(3)
    across(2)
    arrive(4)
    for i, off in enumerate(order):
        far = w_rows(k, mod4(y + 2), mod4(zh + off))
        recv(far, ("wy", 2, i))
        send(far, far, ("wk", 2, i), sib)
    across(3)
    across(4)
    for rel in (0, -1, 1, 2):
        for i, off in enumerate(order):
            recv(w_rows(o, mod4(y + rel), mod4(zh + off)), ("wk", rel, i))

    for n, rel in enumerate((0, -1, 1, 2)):
        blk = mod4(x + rel)
        if rel == 2:
            for step in range(5):
                for a in range(2):
                    for zrel, _ in steps[step]:
                        recv(shard(a, blk, mod8(z + zrel)), ("x", 2, zrel, a))
        for a in range(2):
            term = lax.dot_general(
                W[a, blk], X[a, blk], (((0,), (0,)), ((), ())), preferred_element_type=F32
            )
            if n == 0:
                H[a] = term
            else:
                H[a] += term

    @pl.loop(0, 6)
    def _(i):
        rows = pl.ds(pl.multiple_of(i * 64, 64), 64)
        active, slope = gelu_pair(H[0, rows, :])
        hb[0, rows, :] = (H[1, rows, :] * slope).astype(BF16)
        hb[1, rows, :] = active.astype(BF16)

    pieces = [(hf, r) for r in range(2) for hf in range(2)]

    def ig_dot(blk, hf, r):
        return jnp.dot(
            W[0, blk, r * 384 : (r + 1) * 384, :],
            hb[0, :, hf * 256 : (hf + 1) * 256],
            preferred_element_type=F32,
        )

    def dw_dot(a, blk, rows):
        return lax.dot_general(
            X[a, blk, rows, :], hb[a], (((1,), (1,)), ((), ())), preferred_element_type=F32
        )

    def ig_send(stage, hf, r, value, device):
        igs[stage, hf, r] = value.astype(BF16)
        send(igs.at[stage, hf, r], igr.at[stage, hf, r], ("ig", stage, hf, r), device)

    def ig_recv(stage, hf, r):
        recv(igr.at[stage, hf, r], ("ig", stage, hf, r))
        return igr[stage, hf, r].astype(F32)

    y_rels = (2, 1, -1, 0)

    def dw_other(n):
        blk = mod4(y + y_rels[n])
        for i in range(2):
            rows = slice(i * 384, (i + 1) * 384)
            ds[n, rows, :] = dw_dot(o, blk, rows).astype(BF16)
            send(ds.at[n, rows, :], dr.at[n, rows, :], ("dk", n, i), sib)

    got = set()

    def dw_own(n, hf, j):
        if (n, hf) not in got:
            rows = slice(hf * 384, (hf + 1) * 384)
            recv(dr.at[n, rows, :], ("dk", n, hf))
            got.add((n, hf))
        rows = slice((2 * hf + j) * 192, (2 * hf + j + 1) * 192)
        return dw_dot(k, mod4(y + y_rels[n]), rows) + dr[n, rows, :].astype(F32)

    def dw_send(stage, hf, j, value, device):
        dws[stage, hf, j] = value.astype(BF16)
        send(dws.at[stage, hf, j], dwr.at[stage, hf, j], ("dw", stage, hf, j), device)

    def dw_recv(stage, hf, j):
        recv(dwr.at[stage, hf, j], ("dw", stage, hf, j))
        return dwr[stage, hf, j].astype(F32)

    for hf, r in pieces:
        ig_send(0, hf, r, ig_dot(mod4(x + 2), hf, r), xm if hf else xp)
    dw_other(0)
    for hf, r in pieces:
        ig_send(1, hf, r, ig_dot(mod4(x + 1 if hf else x - 1), hf, r), xp if hf else xm)
    dw_other(1)
    dw_other(2)
    for hf, j in pieces:
        dw_send(0, hf, j, dw_own(0, hf, j), ym if hf else yp)
    dw_other(3)
    for hf, j in pieces:
        dw_send(1, hf, j, dw_own(1 if hf else 2, hf, j), yp if hf else ym)
    for hf, r in pieces:
        value = ig_dot(mod4(x - 1 if hf else x + 1), hf, r) + ig_recv(0, hf, r)
        ig_send(2, hf, r, value, xm if hf else xp)
    for hf, j in pieces:
        value = dw_own(2 if hf else 1, hf, j) + dw_recv(0, hf, j)
        dw_send(2, hf, j, value, ym if hf else yp)

    z_base = recv_no("zr", 8)
    for hf, r in pieces:
        value = ig_dot(x, hf, r) + ig_recv(1, hf, r) + ig_recv(2, hf, r)
        for j in range(2):
            zt = 2 * (2 * hf + j) + r
            block = value[:, j * 128 : (j + 1) * 128]
            zs[zt] = block.astype(BF16)
            copy = copy_to(zs.at[zt], zr.at[z], ("zs", zt), dev(zz=zt), z_base + z)

            @pl.when(zt == z)
            def _():
                own_sum[...] = block

            @pl.when(zt != z)
            def _():
                copy.start()

            sent.append((zt != z, copy))

    d_base = recv_no("dl", 4)

    def dw_place(a, h):
        return dw_out.at[a, :, pl.ds(pl.multiple_of(h * 384, 128), 384)]

    for hf, j in pieces:
        value = dw_own(3, hf, j) + dw_recv(1, hf, j) + dw_recv(2, hf, j)
        zf = 2 * hf + j
        dwl[zf] = value.astype(BF16)
        half = lax.rem(zh, 2)
        send_unless(
            jnp.logical_and(zf == zh, lax.div(zh, 2) == k),
            dwl.at[zf],
            dw_place(k, half),
            ("dl", zf),
            dev(zz=2 * zf + zl, core=lax.div(zh, 2)),
            d_base + 2 * k + half,
        )

    total = own_sum[...]
    for rel in (1, 7, 2, 6, 3, 5, 4):
        zz = mod8(z + rel)
        recv(zr.at[zz], at=z_base + zz)
        total = total + zr[zz].astype(F32)
    last[...] = total.astype(BF16)
    lanes = pl.ds(pl.multiple_of(k * 128, 128), 128)
    half = lambda core: last.at[pl.ds(pl.multiple_of(core * 192, 192), 192), :]
    send(half(o), ig_out.at[:, lanes], ("last",), sib)
    copy = pltpu.make_async_copy(half(k), ig_out.at[:, lanes], local_sems.at[2])
    copy.start()
    recv(ig_out.at[:, pl.ds(pl.multiple_of(o * 128, 128), 128)], ("last",))
    copy.wait()
    for a in range(2):
        for h in range(2):
            recv(dw_place(a, h), at=d_base + 2 * a + h)
    for cond, copy in sent:
        if cond is None:
            copy.wait_send()
        else:

            @pl.when(cond)
            def _():
                copy.wait_send()

    assert max(send_no.count, recv_no.count) <= SEMS


def body(tokens, out_grad, w_up, w_down):
    any_ = pl.BlockSpec(memory_space=pl.ANY)
    dw, ig = pl.pallas_call(
        kernel,
        out_shape=(
            jax.ShapeDtypeStruct((2, 192, 768), BF16),
            jax.ShapeDtypeStruct((192, 256), BF16),
        ),
        in_specs=[any_] * 4,
        out_specs=(any_, any_),
        scratch_shapes=[
            pltpu.VMEM((2, 4, 768, 512), BF16),
            pltpu.VMEM((2, 4, 768, 384), BF16),
            pltpu.VMEM((2, 384, 512), F32),
            pltpu.VMEM((2, 384, 512), BF16),
            pltpu.VMEM((3, 2, 2, 384, 256), BF16),
            pltpu.VMEM((3, 2, 2, 384, 256), BF16),
            pltpu.VMEM((8, 384, 128), BF16),
            pltpu.VMEM((8, 384, 128), BF16),
            pltpu.VMEM((384, 128), F32),
            pltpu.VMEM((384, 128), BF16),
            pltpu.VMEM((4, 768, 384), BF16),
            pltpu.VMEM((4, 768, 384), BF16),
            pltpu.VMEM((3, 2, 2, 192, 384), BF16),
            pltpu.VMEM((3, 2, 2, 192, 384), BF16),
            pltpu.VMEM((4, 192, 384), BF16),
            pltpu.SemaphoreType.DMA((SEMS,)),
            pltpu.SemaphoreType.DMA((SEMS,)),
            pltpu.SemaphoreType.DMA((4,)),
        ],
        compiler_params=pltpu.CompilerParams(
            collective_id=0, has_side_effects=True, vmem_limit_bytes=58 * 2**20
        ),
        cost_estimate=pl.CostEstimate(
            flops=6 * 10**9, bytes_accessed=4 * 10**6, transcendentals=2 * 10**5
        ),
        name="ffn_backward",
    )(tokens.T, out_grad.T, w_up, w_down)
    factor = 1.0 / math.sqrt(tokens.shape[0] * lax.axis_size("row"))
    grads = dw.astype(F32) * factor
    return (ig.T, grads[0], grads[1])


def solution(mesh):
    return jax.shard_map(
        body,
        mesh=mesh,
        in_specs=(P("row", "col"), P("row", "col"), P("row", "col"), P("row", "col")),
        out_specs=(P("row", "col"), P("row", "col"), P("row", "col")),
        check_vma=False,
    )
```

```python
import math

import jax
import jax.numpy as jnp
from jax import lax
from jax.experimental import pallas as pl
from jax.experimental.pallas import tpu as pltpu
from jax.sharding import PartitionSpec as P

gelu_coef = math.sqrt(2.0 / math.pi)
cubic_coef = 0.044715
MESH = pl.DeviceIdType.MESH
BF16 = jnp.bfloat16
F32 = jnp.float32


def gelu_pair(hidden):
    inner = gelu_coef * (hidden + cubic_coef * hidden * hidden * hidden)
    tangent = jnp.tanh(inner)
    active = 0.5 * hidden * (1.0 + tangent)
    slope = 0.5 * (1.0 + tangent) + 0.5 * hidden * (1.0 - tangent * tangent) * gelu_coef * (
        1.0 + 3.0 * cubic_coef * hidden * hidden
    )
    return (active, slope)


class Slots:
    def __init__(self):
        self.at = {}
        self.count = 0

    def __call__(self, key, extent=1):
        if key not in self.at:
            self.at[key] = self.count
            self.count += extent
        return self.at[key]


SEMS = 256


def kernel(
    tok, og, wu, wd, dw_out, ig_out,
    X, W, H, hb, igb, igf, igs, igr, zs, zr, own_sum, last, ds, dr, df, dws, dwr, dwl,
    send_sems, recv_sems, local_sems,
):
    row, col = lax.axis_index("row"), lax.axis_index("col")
    x, y = lax.div(col, 4), lax.div(row, 4)
    zh, zl, k = lax.rem(row, 4), lax.rem(lax.div(col, 2), 2), lax.rem(col, 2)
    z = 2 * zh + zl
    o = 1 - k
    mod4 = lambda v: lax.rem(v + 8, 4)
    mod8 = lambda v: lax.rem(v + 16, 8)

    def dev(dx=0, dy=0, zz=None, core=None):
        zz = z if zz is None else zz
        core = k if core is None else core
        xx = mod4(x + dx) if dx else x
        yy = mod4(y + dy) if dy else y
        return (yy * 4 + lax.div(zz, 2), xx * 4 + lax.rem(zz, 2) * 2 + core)

    sib = dev(core=o)
    xp, xm = dev(dx=1), dev(dx=-1)
    yp, ym = dev(dy=1), dev(dy=-1)
    zp, zm = dev(zz=mod8(z + 1)), dev(zz=mod8(z - 1))

    barrier = pltpu.get_barrier_semaphore()
    partners = [sib, xp, xm, yp, ym, zp, zm]
    for rel in (2, 4, 6):
        for core in (k, o):
            partners.append(dev(zz=mod8(z + rel), core=core))
    for partner in partners:
        pl.semaphore_signal(barrier, inc=1, device_id=partner, device_id_type=MESH)
    pl.semaphore_wait(barrier, len(partners))

    send_no, recv_no, local_no = Slots(), Slots(), Slots()
    sent = []

    def copy_to(src, dst, key, device, recv_at=None):
        recv_at = recv_no(key) if recv_at is None else recv_at
        return pltpu.make_async_remote_copy(
            src_ref=src,
            dst_ref=dst,
            send_sem=send_sems.at[send_no(key)],
            recv_sem=recv_sems.at[recv_at],
            device_id=device,
            device_id_type=MESH,
        )

    def send(src, dst, key, device, recv_at=None):
        copy = copy_to(src, dst, key, device, recv_at)
        copy.start()
        sent.append((None, copy))

    def send_unless(own, src, dst, key, device, recv_at):
        copy = copy_to(src, dst, key, device, recv_at)
        local = pltpu.make_async_copy(src, dst, recv_sems.at[recv_at])

        @pl.when(own)
        def _():
            local.start()

        @pl.when(jnp.logical_not(own))
        def _():
            copy.start()

        sent.append((jnp.logical_not(own), copy))

    def recv(dst, key=None, at=None):
        at = recv_no(key) if at is None else at
        pltpu.make_async_remote_copy(
            src_ref=dst,
            dst_ref=dst,
            send_sem=send_sems.at[0],
            recv_sem=recv_sems.at[at],
            device_id=sib,
            device_id_type=MESH,
        ).wait_recv()

    def w_rows(a, yy, zz):
        return W.at[a, yy, pl.ds(pl.multiple_of(zz * 192, 192), 192), :]

    w_base = recv_no("w", 4)
    for h in range(2):
        for a, src in enumerate((wu, wd)):
            zt = 2 * k + h
            send_unless(
                jnp.logical_and(zt == zh, k == a),
                src.at[:, h * 384 : (h + 1) * 384],
                w_rows(a, y, zh),
                ("w", h, a),
                dev(zz=2 * zt + zl, core=a),
                w_base + zh,
            )

    def shard(a, xx, zz):
        return X.at[
            a, xx,
            pl.ds(pl.multiple_of(lax.rem(zz, 2) * 384, 384), 384),
            pl.ds(pl.multiple_of(lax.div(zz, 2) * 128, 128), 128),
        ]

    def part(a, core):
        return X.at[
            a, x,
            pl.ds(pl.multiple_of(zl * 384 + core * 192, 192), 192),
            pl.ds(pl.multiple_of(zh * 128, 128), 128),
        ]

    mine = pl.ds(pl.multiple_of(k * 128, 128), 128)
    other = pl.ds(pl.multiple_of(o * 128, 128), 128)
    locals_ = []
    for a, src in enumerate((tok, og)):
        send(src.at[:, other], part(a, k), ("half", a), sib)
        copy = pltpu.make_async_copy(src.at[:, mine], part(a, k), local_sems.at[a])
        copy.start()
        locals_.append(copy)
    for a in range(2):
        locals_[a].wait()
        recv(part(a, o), ("half", a))

    steps = [[(0, 0)], [(-1, 1), (1, -1)], [(-2, 1), (2, -1)], [(-3, 1), (3, -1)], [(4, 0)]]

    def arrive(step):
        for a in range(2):
            for rel, way in steps[step]:
                block = shard(a, x, mod8(z + rel))
                if step == 0:
                    send(block, block, ("z", -1, a), zp)
                    send(block, block, ("z", 1, a), zm)
                else:
                    recv(block, ("z", rel, a))
                    if way == 1 and (step < 3 or (step == 3 and a == 0)):
                        send(block, block, ("z", rel - 1 if step < 3 else 4, a), zp)
                    if way == -1 and (step < 3 or (step == 3 and a == 1)):
                        send(block, block, ("z", rel + 1 if step < 3 else 4, a), zm)
                send(block, block, ("x", -1, rel, a), xp)
                send(block, block, ("x", 1, rel, a), xm)

    def across(step):
        for a in range(2):
            for rel, _ in steps[step]:
                zz = mod8(z + rel)
                left, right = shard(a, mod4(x - 1), zz), shard(a, mod4(x + 1), zz)
                recv(left, ("x", -1, rel, a))
                if a == 0:
                    send(left, left, ("x", 2, rel, a), xp)
                recv(right, ("x", 1, rel, a))
                if a == 1:
                    send(right, right, ("x", 2, rel, a), xm)

    order = [0, 1, 3, 2]
    arrive(0)

    for i, off in enumerate(order):
        zz = mod4(zh + off)
        block = w_rows(k, y, zz)
        recv(block, at=w_base + zz)
        send(block, block, ("wy", -1, i), yp)
        send(block, block, ("wy", 1, i), ym)
        send(block, block, ("wk", 0, i), sib)
        if i == 1:
            arrive(1)
    for i, off in enumerate(order):
        zz = mod4(zh + off)
        left, right = w_rows(k, mod4(y - 1), zz), w_rows(k, mod4(y + 1), zz)
        recv(left, ("wy", -1, i))
        if i < 2:
            send(left, left, ("wy", 2, i), yp)
        send(left, left, ("wk", -1, i), sib)
        recv(right, ("wy", 1, i))
        if i >= 2:
            send(right, right, ("wy", 2, i), ym)
        send(right, right, ("wk", 1, i), sib)
        if i == 0:
            across(0)
            arrive(2)
        if i == 2:
            across(1)
            arrive(3)
    across(2)
    arrive(4)
    for i, off in enumerate(order):
        far = w_rows(k, mod4(y + 2), mod4(zh + off))
        recv(far, ("wy", 2, i))
        send(far, far, ("wk", 2, i), sib)
    across(3)
    across(4)
    for rel in (0, -1, 1, 2):
        for i, off in enumerate(order):
            recv(w_rows(o, mod4(y + rel), mod4(zh + off)), ("wk", rel, i))

    for n, rel in enumerate((0, -1, 1, 2)):
        blk = mod4(x + rel)
        if rel == 2:
            for step in range(5):
                for a in range(2):
                    for zrel, _ in steps[step]:
                        recv(shard(a, blk, mod8(z + zrel)), ("x", 2, zrel, a))
        for a in range(2):
            term = lax.dot_general(
                W[a, blk], X[a, blk], (((0,), (0,)), ((), ())), preferred_element_type=F32
            )
            if n == 0:
                H[a] = term
            else:
                H[a] += term

    @pl.loop(0, 6)
    def _(i):
        rows = pl.ds(pl.multiple_of(i * 64, 64), 64)
        active, slope = gelu_pair(H[0, rows, :])
        hb[0, rows, :] = (H[1, rows, :] * slope).astype(BF16)
        hb[1, rows, :] = active.astype(BF16)

    def rows_of(start, size, align):
        return pl.ds(pl.multiple_of(start, align), size)

    def ig_block(rel):
        for i in range(3):
            rows = slice(i * 256, (i + 1) * 256)
            value = jnp.dot(W[0, mod4(x + rel), rows, :], hb[0], preferred_element_type=F32)
            if rel != 0:
                igb[rel % 4, rows, :] = value.astype(BF16)
            if rel != 2:
                igf[rel % 4, rows, :] = value

    def ig_spot(g, t):
        zt = mod8(z + (4 - g) * (1, -1)[t])
        whole = 0 < g < 4
        start = lax.rem(zt, 2) * 384 + (0 if whole else 192 * t)
        rows = rows_of(start, 384 if whole else 192, 192)
        return rows, rows_of(lax.div(zt, 2) * 128, 128, 128)

    def height(g):
        return slice(0, 384 if 0 < g < 4 else 192)

    def ig_s1(g):
        for t in range(2):
            send(
                igb.at[(2, *ig_spot(g, t))], igr.at[0, g, t, height(g)],
                ("ig", 0, g, t), (xp, xm)[t],
            )

    def ig_s2(g):
        for t in range(2):
            send(
                igb.at[((3, 1)[t], *ig_spot(g, t))], igr.at[1, g, t, height(g)],
                ("ig", 1, g, t), (xm, xp)[t],
            )

    def ig_recv(stage, g, t):
        recv(igr.at[stage, g, t, height(g)], ("ig", stage, g, t))
        return igr[stage, g, t, height(g), :].astype(F32)

    def ig_s3(g):
        for t in range(2):
            value = igf[((1, 3)[t], *ig_spot(g, t))] + ig_recv(0, g, t)
            igs[g, t, height(g), :] = value.astype(BF16)
            send(
                igs.at[g, t, height(g)], igr.at[2, g, t, height(g)],
                ("ig", 2, g, t), (xp, xm)[t],
            )

    def zc_recv(g, t):
        recv(zr.at[g, t, height(g)], ("zc", g, t))
        return zr[g, t, height(g), :].astype(F32)

    def ig_s4(g):
        for t in range(2):
            value = igf[(0, *ig_spot(g, t))] + ig_recv(1, g, t) + ig_recv(2, g, t)
            if g == 4:
                own_sum[192 * t : 192 * (t + 1), :] = value
                continue
            if g > 1:
                value = value + zc_recv(g - 1, t)
            zs[g, t, height(g), :] = value.astype(BF16)
            if g == 1:
                part_rows = slice(192 * t, 192 * (t + 1))
                summed = value[part_rows] + zc_recv(0, t)
                zs[g, t, part_rows, :] = summed.astype(BF16)
            send(
                zs.at[g, t, height(g)], zr.at[g, t, height(g)],
                ("zc", g, t), (zp, zm)[t],
            )

    def dw_block(a, rel, rows):
        return lax.dot_general(
            X[a, mod4(y + rel), rows, :], hb[a], (((1,), (1,)), ((), ())),
            preferred_element_type=F32,
        )

    def dw_other(rel):
        for i in range(2):
            rows = slice(i * 384, (i + 1) * 384)
            ds[rel % 4, rows, :] = dw_block(o, rel, rows).astype(BF16)
            send(ds.at[rel % 4, rows, :], dr.at[rel % 4, rows, :], ("dk", rel, i), sib)

    def dw_own(rel):
        for i in range(2):
            rows = slice(i * 384, (i + 1) * 384)
            df[rel % 4, rows, :] = dw_block(k, rel, rows)

    def dw_sum(rel):
        for i in range(2):
            recv(dr.at[rel % 4, i * 384 : (i + 1) * 384, :], ("dk", rel, i))

    def dw_value(rel, q, t):
        rows = slice(384 * t + 96 * q, 384 * t + 96 * (q + 1))
        return df[rel % 4, rows, :] + dr[rel % 4, rows, :].astype(F32)

    def dw_send(stage, q, t, value, device):
        dws[stage, q, t] = value.astype(BF16)
        send(dws.at[stage, q, t], dwr.at[stage, q, t], ("dw", stage, q, t), device)

    def dw_recv(stage, q, t):
        recv(dwr.at[stage, q, t], ("dw", stage, q, t))
        return dwr[stage, q, t].astype(F32)

    def dw_s1(q):
        for t in range(2):
            dw_send(0, q, t, dw_value(2, q, t), (yp, ym)[t])

    def dw_s2(q):
        for t in range(2):
            dw_send(1, q, t, dw_value((-1, 1)[t], q, t), (ym, yp)[t])

    def dw_s3(q):
        for t in range(2):
            dw_send(2, q, t, dw_value((1, -1)[t], q, t) + dw_recv(0, q, t), (yp, ym)[t])

    d_base = recv_no("dl", 8)

    def dw_place(a, h, q):
        return dw_out.at[
            a, 96 * (q % 2) : 96 * (q % 2 + 1), pl.ds(pl.multiple_of(h * 384, 128), 384)
        ]

    def dw_s4(q):
        for t in range(2):
            value = dw_value(0, q, t) + dw_recv(1, q, t) + dw_recv(2, q, t)
            dwl[q, t] = value.astype(BF16)
            zf = 2 * t + q // 2
            half = lax.rem(zh, 2)
            send_unless(
                jnp.logical_and(zf == zh, lax.div(zh, 2) == k),
                dwl.at[q, t],
                dw_place(k, half, q),
                ("dl", q, t),
                dev(zz=2 * zf + zl, core=lax.div(zh, 2)),
                d_base + 2 * (2 * k + half) + q % 2,
            )

    ig_block(2)
    ig_s1(0)
    ig_s1(1)
    dw_other(2)
    ig_block(1)
    ig_block(-1)
    ig_s2(0)
    ig_s2(1)
    dw_own(2)
    dw_other(1)
    dw_other(-1)
    dw_sum(2)
    dw_s1(0)
    dw_s1(1)
    dw_own(1)
    dw_own(-1)
    dw_sum(1)
    dw_sum(-1)
    dw_s2(0)
    dw_s2(1)
    ig_block(0)
    dw_other(0)
    dw_own(0)
    dw_sum(0)
    ig_s3(0)
    ig_s1(2)
    ig_s2(2)
    dw_s3(0)
    dw_s1(2)
    dw_s2(2)
    ig_s3(1)
    ig_s1(3)
    ig_s2(3)
    ig_s4(0)
    dw_s3(1)
    dw_s1(3)
    dw_s2(3)
    dw_s4(0)
    ig_s3(2)
    ig_s1(4)
    ig_s2(4)
    ig_s4(1)
    dw_s3(2)
    dw_s4(1)
    ig_s3(3)
    ig_s4(2)
    dw_s3(3)
    dw_s4(2)
    ig_s3(4)
    ig_s4(3)
    dw_s4(3)
    ig_s4(4)

    last[...] = (own_sum[...] + zc_recv(3, 0) + zc_recv(3, 1)).astype(BF16)
    lanes = pl.ds(pl.multiple_of(k * 128, 128), 128)
    half = lambda core: last.at[pl.ds(pl.multiple_of(core * 192, 192), 192), :]
    send(half(o), ig_out.at[:, lanes], ("last",), sib)
    copy = pltpu.make_async_copy(half(k), ig_out.at[:, lanes], local_sems.at[2])
    copy.start()
    recv(ig_out.at[:, pl.ds(pl.multiple_of(o * 128, 128), 128)], ("last",))
    copy.wait()
    for a in range(2):
        for h in range(2):
            for q in range(2):
                recv(dw_place(a, h, q), at=d_base + 2 * (2 * a + h) + q)
    for cond, copy in sent:
        if cond is None:
            copy.wait_send()
        else:

            @pl.when(cond)
            def _():
                copy.wait_send()

    assert max(send_no.count, recv_no.count) <= SEMS


def body(tokens, out_grad, w_up, w_down):
    any_ = pl.BlockSpec(memory_space=pl.ANY)
    dw, ig = pl.pallas_call(
        kernel,
        out_shape=(
            jax.ShapeDtypeStruct((2, 192, 768), BF16),
            jax.ShapeDtypeStruct((192, 256), BF16),
        ),
        in_specs=[any_] * 4,
        out_specs=(any_, any_),
        scratch_shapes=[
            pltpu.VMEM((2, 4, 768, 512), BF16),
            pltpu.VMEM((2, 4, 768, 384), BF16),
            pltpu.VMEM((2, 384, 512), F32),
            pltpu.VMEM((2, 384, 512), BF16),
            pltpu.VMEM((4, 768, 512), BF16),
            pltpu.VMEM((4, 768, 512), F32),
            pltpu.VMEM((5, 2, 384, 128), BF16),
            pltpu.VMEM((3, 5, 2, 384, 128), BF16),
            pltpu.VMEM((4, 2, 384, 128), BF16),
            pltpu.VMEM((4, 2, 384, 128), BF16),
            pltpu.VMEM((384, 128), F32),
            pltpu.VMEM((384, 128), BF16),
            pltpu.VMEM((4, 768, 384), BF16),
            pltpu.VMEM((4, 768, 384), BF16),
            pltpu.VMEM((4, 768, 384), F32),
            pltpu.VMEM((3, 4, 2, 96, 384), BF16),
            pltpu.VMEM((3, 4, 2, 96, 384), BF16),
            pltpu.VMEM((4, 2, 96, 384), BF16),
            pltpu.SemaphoreType.DMA((SEMS,)),
            pltpu.SemaphoreType.DMA((SEMS,)),
            pltpu.SemaphoreType.DMA((4,)),
        ],
        compiler_params=pltpu.CompilerParams(
            collective_id=0, has_side_effects=True, vmem_limit_bytes=58 * 2**20
        ),
        cost_estimate=pl.CostEstimate(
            flops=6 * 10**9, bytes_accessed=4 * 10**6, transcendentals=2 * 10**5
        ),
        name="ffn_backward",
    )(tokens.T, out_grad.T, w_up, w_down)
    factor = 1.0 / math.sqrt(tokens.shape[0] * lax.axis_size("row"))
    return (ig.T, dw[0].astype(F32) * factor, dw[1].astype(F32) * factor)


def solution(mesh):
    return jax.shard_map(
        body,
        mesh=mesh,
        in_specs=(P("row", "col"), P("row", "col"), P("row", "col"), P("row", "col")),
        out_specs=(P("row", "col"), P("row", "col"), P("row", "col")),
        check_vma=False,
    )
```

```python
import math

import jax
import jax.numpy as jnp
from jax import lax
from jax.experimental import pallas as pl
from jax.experimental.pallas import tpu as pltpu
from jax.sharding import PartitionSpec as P

gelu_coef = math.sqrt(2.0 / math.pi)
cubic_coef = 0.044715
MESH = pl.DeviceIdType.MESH
BF16 = jnp.bfloat16
F32 = jnp.float32


def gelu_pair(hidden):
    inner = gelu_coef * (hidden + cubic_coef * hidden * hidden * hidden)
    tangent = jnp.tanh(inner)
    active = 0.5 * hidden * (1.0 + tangent)
    slope = 0.5 * (1.0 + tangent) + 0.5 * hidden * (1.0 - tangent * tangent) * gelu_coef * (
        1.0 + 3.0 * cubic_coef * hidden * hidden
    )
    return (active, slope)


class Slots:
    def __init__(self):
        self.at = {}
        self.count = 0
        self.bytes = {}

    def __call__(self, key, extent=1):
        if key not in self.at:
            self.at[key] = self.count
            self.count += extent
        return self.at[key]

    def add(self, key, size):
        self.bytes[key] = self.bytes.get(key, 0) + size
        return self(key)


SENDS = 13
RECVS = 76
BLOCK = 192 * 384 * 2


def kernel(
    tok, og, wu, wd, dw_out, ig_out,
    X, W, H, hb, igb, igf, igs, igr, zs, zr, own_sum, last, ds, dr, df, dws, dwr, dwl,
    send_sems, recv_sems, local_sems,
):
    row, col = lax.axis_index("row"), lax.axis_index("col")
    x, y = lax.div(col, 4), lax.div(row, 4)
    zh, zl, k = lax.rem(row, 4), lax.rem(lax.div(col, 2), 2), lax.rem(col, 2)
    z = 2 * zh + zl
    o = 1 - k
    mod4 = lambda v: lax.rem(v + 8, 4)
    mod8 = lambda v: lax.rem(v + 16, 8)

    def dev(dx=0, dy=0, zz=None, core=None):
        zz = z if zz is None else zz
        core = k if core is None else core
        xx = mod4(x + dx) if dx else x
        yy = mod4(y + dy) if dy else y
        return (yy * 4 + lax.div(zz, 2), xx * 4 + lax.rem(zz, 2) * 2 + core)

    sib = dev(core=o)
    xp, xm = dev(dx=1), dev(dx=-1)
    yp, ym = dev(dy=1), dev(dy=-1)
    zp, zm = dev(zz=mod8(z + 1)), dev(zz=mod8(z - 1))

    def part(a, core):
        return X.at[
            a, x,
            pl.ds(pl.multiple_of(zl * 384 + core * 192, 192), 192),
            pl.ds(pl.multiple_of(zh * 128, 128), 128),
        ]

    mine = pl.ds(pl.multiple_of(k * 128, 128), 128)
    other = pl.ds(pl.multiple_of(o * 128, 128), 128)
    kept = [
        pltpu.make_async_copy(src.at[:, mine], part(a, k), local_sems.at[a])
        for a, src in enumerate((tok, og))
    ]
    for copy in kept:
        copy.start()

    barrier = pltpu.get_barrier_semaphore()
    partners = [sib, xp, xm, yp, ym, zp, zm]
    for rel in (2, 4, 6):
        for core in (k, o):
            partners.append(dev(zz=mod8(z + rel), core=core))
    for partner in partners:
        pl.semaphore_signal(barrier, inc=1, device_id=partner, device_id_type=MESH)
    pl.semaphore_wait(barrier, len(partners))

    send_no, recv_no = Slots(), Slots()

    def size_of(ref):
        return math.prod(ref.shape) * 2

    def view(size):
        for lead in (1, 2, 3, 4, 6, 8):
            rows, rest = divmod(size, lead * 1024)
            if rest == 0 and rows <= 768 and rows % 16 == 0:
                if lead < 5:
                    return X.at[0, :lead, :rows, :]
                return X.at[:, : lead // 2, :rows, :]
        for rows in range(768, 0, -16):
            for lead in (1, 2, 3, 4):
                if size == lead * rows * 256:
                    return X.at[0, :lead, :rows, :128]
        raise ValueError(size)

    def dummy(size, send_at=0, recv_at=0):
        return pltpu.make_async_remote_copy(
            src_ref=view(size),
            dst_ref=view(size),
            send_sem=send_sems.at[send_at],
            recv_sem=recv_sems.at[recv_at],
            device_id=sib,
            device_id_type=MESH,
        )

    def send(src, dst, group, key, device):
        size = size_of(src)
        pltpu.make_async_remote_copy(
            src_ref=src,
            dst_ref=dst,
            send_sem=send_sems.at[send_no.add(group, size)],
            recv_sem=recv_sems.at[recv_no.add(key, size)],
            device_id=device,
            device_id_type=MESH,
        ).start()

    def send_unless(own, src, dst, group, device, recv_at):
        copy = pltpu.make_async_remote_copy(
            src_ref=src,
            dst_ref=dst,
            send_sem=send_sems.at[send_no(group)],
            recv_sem=recv_sems.at[recv_at],
            device_id=device,
            device_id_type=MESH,
        )
        local = pltpu.make_async_copy(src, dst, recv_sems.at[recv_at])

        @pl.when(own)
        def _():
            local.start()

        @pl.when(jnp.logical_not(own))
        def _():
            copy.start()

    def recv(key):
        dummy(recv_no.bytes[key], recv_at=recv_no(key)).wait_recv()

    def w_rows(a, yy, zz):
        return W.at[a, yy, pl.ds(pl.multiple_of(zz * 192, 192), 192), :]

    w_base = recv_no("w", 4)

    def w_out(a):
        for h in range(2):
            zt = 2 * k + h
            send_unless(
                jnp.logical_and(zt == zh, k == a),
                (wu, wd)[a].at[:, h * 384 : (h + 1) * 384],
                w_rows(a, y, zh),
                "w",
                dev(zz=2 * zt + zl, core=a),
                w_base + zh,
            )

    for a, src in enumerate((tok, og)):
        send(src.at[:, other], part(a, k), "half", "half", sib)
    w_out(0)
    w_out(1)

    def lanes_of(zz):
        return pl.ds(pl.multiple_of(lax.div(zz, 2) * 128, 128), 128)

    def tok_shard(xx, zz):
        start = lax.rem(zz, 2) * 384
        return X.at[0, xx, pl.ds(pl.multiple_of(start, 384), 384), lanes_of(zz)]

    def og_shard(xx, zz):
        start = lax.rem(zz, 2) * 384
        return X.at[1, xx, pl.ds(pl.multiple_of(start, 384), 192), lanes_of(zz)]

    def rest_shard(xx, start, size):
        first = zl * 384 + 192 + start
        return X.at[1, xx, pl.ds(pl.multiple_of(first, 96), size), lanes_of(z)]

    def rest_shards(xs, zz):
        first = lax.rem(zz, 2) * 384 + 192
        return X.at[1, xs, pl.ds(pl.multiple_of(first, 192), 192), lanes_of(zz)]

    steps = [[0], [-1, 1], [-2, 2], [-3, 3], [4]]

    def arrive(step):
        for rel in steps[step]:
            blocks = [tok_shard(x, mod8(z + rel)), og_shard(x, mod8(z + rel))]
            if step > 0:
                recv(("z", rel))
            for n, block in enumerate(blocks):
                if step < 3 and rel <= 0:
                    send(block, block, "z", ("z", rel - 1), zp)
                if step < 3 and rel >= 0:
                    send(block, block, "z", ("z", rel + 1), zm)
                if rel == -3 and n == 0:
                    send(block, block, "z", ("z", 4), zp)
                if rel == 3 and n == 1:
                    send(block, block, "z", ("z", 4), zm)
            for block in blocks:
                send(block, block, "x", ("x", -1, rel), xp)
                send(block, block, "x", ("x", 1, rel), xm)

    def across(step):
        for rel in steps[step]:
            zz = mod8(z + rel)
            shards = (tok_shard, og_shard) if rel % 2 == 0 else (og_shard, tok_shard)
            left, right = shards[0](mod4(x - 1), zz), shards[1](mod4(x + 1), zz)
            recv(("x", -1, rel))
            send(left, left, "x", "far", xp)
            recv(("x", 1, rel))
            send(right, right, "x", "far", xm)

    def rest_x(step):
        if step == 0:
            block = rest_shard(x, 0, 192)
            send(block, block, "rest", "rest near", xp)
            send(block, block, "rest", "rest near", xm)
        if step == 1:
            recv("rest near")
            left, right = rest_shard(mod4(x - 1), 0, 96), rest_shard(mod4(x + 1), 96, 96)
            send(left, left, "rest", "rest far", xp)
            send(right, right, "rest", "rest far", xm)
        if step == 2:
            recv("rest far")

    def rest_z(step):
        for way in (-1, 1):
            if step > 0:
                recv(("rest", way * step))
            if step < 3:
                block = rest_shards(slice(0, 4), mod8(z + way * step))
                send(block, block, "rest", ("rest", way * (step + 1)), zp if way < 0 else zm)
            else:
                xs = slice(0, 2) if way < 0 else slice(2, 4)
                block = rest_shards(xs, mod8(z + way * step))
                send(block, block, "rest", ("rest", 4), zp if way < 0 else zm)

    order = [0, 1, 3, 2]

    def w_in(i):
        zz = mod4(zh + order[i])
        block = w_rows(k, y, zz)
        dummy(BLOCK, recv_at=w_base + zz).wait_recv()
        send(block, block, "wy", ("wy", -1, i), yp)
        send(block, block, "wy", ("wy", 1, i), ym)
        send(block, block, "wk", "wk", sib)

    def w_ring(i):
        zz = mod4(zh + order[i])
        left, right = w_rows(k, mod4(y - 1), zz), w_rows(k, mod4(y + 1), zz)
        recv(("wy", -1, i))
        if i % 2 == 0:
            send(left, left, "wy", "wy far", yp)
        send(left, left, "wk", "wk", sib)
        recv(("wy", 1, i))
        if i % 2 == 1:
            send(right, right, "wy", "wy far", ym)
        send(right, right, "wk", "wk", sib)

    for a in range(2):
        kept[a].wait()
    recv("half")
    arrive(0)
    rest_x(0)
    w_in(0)
    arrive(1)
    rest_x(1)
    across(0)
    rest_x(2)
    rest_z(0)
    w_in(1)
    w_in(2)
    arrive(2)
    w_in(3)
    w_ring(0)
    across(1)
    rest_z(1)
    arrive(3)
    w_ring(1)
    across(2)
    w_ring(2)
    arrive(4)
    rest_z(2)
    w_ring(3)
    across(3)
    rest_z(3)
    recv("wy far")
    far = W.at[k, mod4(y + 2)]
    send(far, far, "wk", "wk", sib)
    across(4)
    recv("wk")

    def hidden_term(a, rel):
        blk = mod4(x + rel)
        term = lax.dot_general(
            W[a, blk], X[a, blk], (((0,), (0,)), ((), ())), preferred_element_type=F32
        )
        if rel == 0:
            H[a] = term
        else:
            H[a] += term

    for rel in (0, -1, 1):
        hidden_term(0, rel)
    recv(("rest", 4))
    for rel in (0, -1, 1):
        hidden_term(1, rel)
    recv("far")
    for a in range(2):
        hidden_term(a, 2)

    @pl.loop(0, 6)
    def _(i):
        rows = pl.ds(pl.multiple_of(i * 64, 64), 64)
        active, slope = gelu_pair(H[0, rows, :])
        hb[0, rows, :] = (H[1, rows, :] * slope).astype(BF16)
        hb[1, rows, :] = active.astype(BF16)

    def rows_of(start, size, align):
        return pl.ds(pl.multiple_of(start, align), size)

    def ig_block(rel):
        for i in range(3):
            rows = slice(i * 256, (i + 1) * 256)
            value = jnp.dot(W[0, mod4(x + rel), rows, :], hb[0], preferred_element_type=F32)
            if rel != 0:
                igb[rel % 4, rows, :] = value.astype(BF16)
            if rel != 2:
                igf[rel % 4, rows, :] = value

    def ig_spot(g, t):
        zt = mod8(z + (4 - g) * (1, -1)[t])
        whole = 0 < g < 4
        start = lax.rem(zt, 2) * 384 + (0 if whole else 192 * t)
        rows = rows_of(start, 384 if whole else 192, 192)
        return rows, rows_of(lax.div(zt, 2) * 128, 128, 128)

    def height(g):
        return slice(0, 384 if 0 < g < 4 else 192)

    def ig_s1(g):
        for t in range(2):
            send(
                igb.at[(2, *ig_spot(g, t))], igr.at[0, g, t, height(g)],
                "ig", ("ig", 0, g), (xp, xm)[t],
            )

    def ig_s2(g):
        for t in range(2):
            send(
                igb.at[((3, 1)[t], *ig_spot(g, t))], igr.at[1, g, t, height(g)],
                "ig", ("ig", 1, g), (xm, xp)[t],
            )

    def ig_got(stage, g, t):
        return igr[stage, g, t, height(g), :].astype(F32)

    def ig_s3(g):
        recv(("ig", 0, g))
        for t in range(2):
            value = igf[((1, 3)[t], *ig_spot(g, t))] + ig_got(0, g, t)
            igs[g, t, height(g), :] = value.astype(BF16)
            send(
                igs.at[g, t, height(g)], igr.at[2, g, t, height(g)],
                "ig", ("ig", 1, g), (xp, xm)[t],
            )

    def zc_got(g, t):
        return zr[g, t, height(g), :].astype(F32)

    def ig_s4(g):
        recv(("ig", 1, g))
        if 0 < g < 4:
            recv(("zc", g - 1))
        for t in range(2):
            value = igf[(0, *ig_spot(g, t))] + ig_got(1, g, t) + ig_got(2, g, t)
            if g == 4:
                own_sum[192 * t : 192 * (t + 1), :] = value
                continue
            if g > 1:
                value = value + zc_got(g - 1, t)
            zs[g, t, height(g), :] = value.astype(BF16)
            if g == 1:
                part_rows = slice(192 * t, 192 * (t + 1))
                summed = value[part_rows] + zc_got(0, t)
                zs[g, t, part_rows, :] = summed.astype(BF16)
            send(
                zs.at[g, t, height(g)], zr.at[g, t, height(g)],
                "zc", ("zc", g), (zp, zm)[t],
            )

    def dw_block(a, rel, rows):
        return lax.dot_general(
            X[a, mod4(y + rel), rows, :], hb[a], (((1,), (1,)), ((), ())),
            preferred_element_type=F32,
        )

    def dw_other(rel):
        for i in range(2):
            rows = slice(i * 384, (i + 1) * 384)
            ds[rel % 4, rows, :] = dw_block(o, rel, rows).astype(BF16)
            send(ds.at[rel % 4, rows, :], dr.at[rel % 4, rows, :], "dk", ("dk", rel), sib)

    def dw_own(rel):
        for i in range(2):
            rows = slice(i * 384, (i + 1) * 384)
            df[rel % 4, rows, :] = dw_block(k, rel, rows)

    def dw_sum(rel):
        recv(("dk", rel))

    def dw_value(rel, q, t):
        rows = slice(384 * t + 96 * q, 384 * t + 96 * (q + 1))
        return df[rel % 4, rows, :] + dr[rel % 4, rows, :].astype(F32)

    def dw_send(stage, q, t, value, device):
        dws[stage, q, t] = value.astype(BF16)
        send(dws.at[stage, q, t], dwr.at[stage, q, t], "dw", ("dw", min(stage, 1), q), device)

    def dw_got(stage, q, t):
        return dwr[stage, q, t].astype(F32)

    def dw_s1(q):
        for t in range(2):
            dw_send(0, q, t, dw_value(2, q, t), (yp, ym)[t])

    def dw_s2(q):
        for t in range(2):
            dw_send(1, q, t, dw_value((-1, 1)[t], q, t), (ym, yp)[t])

    def dw_s3(q):
        recv(("dw", 0, q))
        for t in range(2):
            dw_send(2, q, t, dw_value((1, -1)[t], q, t) + dw_got(0, q, t), (yp, ym)[t])

    d_at = recv_no("dl")

    def dw_place(a, h, q):
        return dw_out.at[
            a, 96 * (q % 2) : 96 * (q % 2 + 1), pl.ds(pl.multiple_of(h * 384, 128), 384)
        ]

    def dw_s4(q):
        recv(("dw", 1, q))
        for t in range(2):
            value = dw_value(0, q, t) + dw_got(1, q, t) + dw_got(2, q, t)
            dwl[q, t] = value.astype(BF16)
            zf = 2 * t + q // 2
            half = lax.rem(zh, 2)
            send_unless(
                jnp.logical_and(zf == zh, lax.div(zh, 2) == k),
                dwl.at[q, t],
                dw_place(k, half, q),
                "dl",
                dev(zz=2 * zf + zl, core=lax.div(zh, 2)),
                d_at,
            )

    ig_block(2)
    ig_s1(0)
    ig_s1(1)
    dw_other(2)
    ig_block(1)
    ig_block(-1)
    ig_s2(0)
    ig_s2(1)
    dw_own(2)
    dw_other(1)
    dw_other(-1)
    dw_sum(2)
    dw_s1(0)
    dw_s1(1)
    dw_own(1)
    dw_own(-1)
    dw_sum(1)
    dw_sum(-1)
    dw_s2(0)
    dw_s2(1)
    ig_block(0)
    dw_other(0)
    dw_own(0)
    dw_sum(0)
    ig_s3(0)
    ig_s1(2)
    ig_s2(2)
    dw_s3(0)
    dw_s1(2)
    dw_s2(2)
    ig_s3(1)
    ig_s1(3)
    ig_s2(3)
    ig_s4(0)
    dw_s3(1)
    dw_s1(3)
    dw_s2(3)
    dw_s4(0)
    ig_s3(2)
    ig_s1(4)
    ig_s2(4)
    ig_s4(1)
    dw_s3(2)
    dw_s4(1)
    ig_s3(3)
    ig_s4(2)
    dw_s3(3)
    dw_s4(2)
    ig_s3(4)
    ig_s4(3)
    dw_s4(3)
    ig_s4(4)

    recv(("zc", 3))
    last[...] = (own_sum[...] + zc_got(3, 0) + zc_got(3, 1)).astype(BF16)
    half = lambda core: last.at[pl.ds(pl.multiple_of(core * 192, 192), 192), :]
    send(half(o), ig_out.at[:, mine], "last", "last", sib)
    copy = pltpu.make_async_copy(half(k), ig_out.at[:, mine], local_sems.at[2])
    copy.start()
    copy.wait()
    recv("last")
    dummy(8 * BLOCK // 2, recv_at=d_at).wait_recv()

    for group, size in send_no.bytes.items():
        dummy(size, send_at=send_no(group)).wait_send()
    some_own = lax.div(zh, 2) == k

    @pl.when(some_own)
    def _():
        dummy(3 * BLOCK, send_at=send_no("w")).wait_send()
        dummy(6 * BLOCK // 2, send_at=send_no("dl")).wait_send()

    @pl.when(jnp.logical_not(some_own))
    def _():
        dummy(4 * BLOCK, send_at=send_no("w")).wait_send()
        dummy(8 * BLOCK // 2, send_at=send_no("dl")).wait_send()

    assert send_no.count <= SENDS and recv_no.count <= RECVS


def body(tokens, out_grad, w_up, w_down):
    any_ = pl.BlockSpec(memory_space=pl.ANY)
    dw, ig = pl.pallas_call(
        kernel,
        out_shape=(
            jax.ShapeDtypeStruct((2, 192, 768), BF16),
            jax.ShapeDtypeStruct((192, 256), BF16),
        ),
        in_specs=[any_] * 4,
        out_specs=(any_, any_),
        scratch_shapes=[
            pltpu.VMEM((2, 4, 768, 512), BF16),
            pltpu.VMEM((2, 4, 768, 384), BF16),
            pltpu.VMEM((2, 384, 512), F32),
            pltpu.VMEM((2, 384, 512), BF16),
            pltpu.VMEM((4, 768, 512), BF16),
            pltpu.VMEM((4, 768, 512), F32),
            pltpu.VMEM((5, 2, 384, 128), BF16),
            pltpu.VMEM((3, 5, 2, 384, 128), BF16),
            pltpu.VMEM((4, 2, 384, 128), BF16),
            pltpu.VMEM((4, 2, 384, 128), BF16),
            pltpu.VMEM((384, 128), F32),
            pltpu.VMEM((384, 128), BF16),
            pltpu.VMEM((4, 768, 384), BF16),
            pltpu.VMEM((4, 768, 384), BF16),
            pltpu.VMEM((4, 768, 384), F32),
            pltpu.VMEM((3, 4, 2, 96, 384), BF16),
            pltpu.VMEM((3, 4, 2, 96, 384), BF16),
            pltpu.VMEM((4, 2, 96, 384), BF16),
            pltpu.SemaphoreType.DMA((SENDS,)),
            pltpu.SemaphoreType.DMA((RECVS,)),
            pltpu.SemaphoreType.DMA((4,)),
        ],
        compiler_params=pltpu.CompilerParams(
            collective_id=0, has_side_effects=True, vmem_limit_bytes=58 * 2**20
        ),
        cost_estimate=pl.CostEstimate(
            flops=6 * 10**9, bytes_accessed=4 * 10**6, transcendentals=2 * 10**5
        ),
        name="ffn_backward",
    )(tokens.T, out_grad.T, w_up, w_down)
    factor = 1.0 / math.sqrt(tokens.shape[0] * lax.axis_size("row"))
    return (ig.T, dw[0].astype(F32) * factor, dw[1].astype(F32) * factor)


def solution(mesh):
    return jax.shard_map(
        body,
        mesh=mesh,
        in_specs=(P("row", "col"), P("row", "col"), P("row", "col"), P("row", "col")),
        out_specs=(P("row", "col"), P("row", "col"), P("row", "col")),
        check_vma=False,
    )
```

```python
import math

import jax
import jax.numpy as jnp
from jax import lax
from jax.experimental import pallas as pl
from jax.experimental.pallas import tpu as pltpu
from jax.sharding import PartitionSpec as P

gelu_coef = math.sqrt(2.0 / math.pi)
cubic_coef = 0.044715
MESH = pl.DeviceIdType.MESH
BF16 = jnp.bfloat16
F32 = jnp.float32


def gelu_pair(hidden):
    inner = gelu_coef * (hidden + cubic_coef * hidden * hidden * hidden)
    tangent = jnp.tanh(inner)
    active = 0.5 * hidden * (1.0 + tangent)
    slope = 0.5 * (1.0 + tangent) + 0.5 * hidden * (1.0 - tangent * tangent) * gelu_coef * (
        1.0 + 3.0 * cubic_coef * hidden * hidden
    )
    return (active, slope)


class Slots:
    def __init__(self):
        self.at = {}
        self.count = 0
        self.bytes = {}

    def __call__(self, key, extent=1):
        if key not in self.at:
            self.at[key] = self.count
            self.count += extent
        return self.at[key]

    def add(self, key, size):
        self.bytes[key] = self.bytes.get(key, 0) + size
        return self(key)


SENDS = 14
RECVS = 86
BLOCK = 192 * 384 * 2
CUT = 98304


def kernel(
    tok, og, wu, wd, dw_out, ig_out,
    X, W, H, hb, igb, igf, igs, igr, zs, zr, own_sum, last, ds, dr, df, dws, dwr, dwl,
    send_sems, recv_sems, local_sems,
):
    row, col = lax.axis_index("row"), lax.axis_index("col")
    x, y = lax.div(col, 4), lax.div(row, 4)
    zh, zl, k = lax.rem(row, 4), lax.rem(lax.div(col, 2), 2), lax.rem(col, 2)
    z = 2 * zh + zl
    o = 1 - k
    mod4 = lambda v: lax.rem(v + 8, 4)
    mod8 = lambda v: lax.rem(v + 16, 8)

    def dev(dx=0, dy=0, zz=None, core=None):
        zz = z if zz is None else zz
        core = k if core is None else core
        xx = mod4(x + dx) if dx else x
        yy = mod4(y + dy) if dy else y
        return (yy * 4 + lax.div(zz, 2), xx * 4 + lax.rem(zz, 2) * 2 + core)

    sib = dev(core=o)
    xp, xm = dev(dx=1), dev(dx=-1)
    yp, ym = dev(dy=1), dev(dy=-1)
    zp, zm = dev(zz=mod8(z + 1)), dev(zz=mod8(z - 1))

    def part(a, core):
        return X.at[
            a, x,
            pl.ds(pl.multiple_of(zl * 384 + core * 192, 192), 192),
            pl.ds(pl.multiple_of(zh * 128, 128), 128),
        ]

    mine = pl.ds(pl.multiple_of(k * 128, 128), 128)
    other = pl.ds(pl.multiple_of(o * 128, 128), 128)
    kept = [
        pltpu.make_async_copy(src.at[:, mine], part(a, k), local_sems.at[a])
        for a, src in enumerate((tok, og))
    ]
    for copy in kept:
        copy.start()

    barrier = pltpu.get_barrier_semaphore()
    partners = [dev(zz=mod8(z + rel), core=core) for rel in (4, 2, 6) for core in (k, o)]
    partners += [xp, xm, yp, ym, zp, zm, sib]
    for partner in partners:
        pl.semaphore_signal(barrier, inc=1, device_id=partner, device_id_type=MESH)
    pl.semaphore_wait(barrier, len(partners))

    send_no, recv_no = Slots(), Slots()

    def size_of(ref):
        return math.prod(ref.shape) * 2

    def view(size):
        for lanes in (512, 384, 256, 128):
            for lead in (1, 2, 3, 4, 6, 8):
                rows, rest = divmod(size, lead * lanes * 2)
                if rest == 0 and rows <= 768 and rows % 16 == 0:
                    if lead < 5:
                        return X.at[0, :lead, :rows, :lanes]
                    return X.at[:, : lead // 2, :rows, :lanes]
        raise ValueError(size)

    def dummy(size, send_at=0, recv_at=0):
        return pltpu.make_async_remote_copy(
            src_ref=view(size),
            dst_ref=view(size),
            send_sem=send_sems.at[send_at],
            recv_sem=recv_sems.at[recv_at],
            device_id=sib,
            device_id_type=MESH,
        )

    def cuts(ref):
        if len(ref.shape) == 3:
            return [piece for n in range(ref.shape[0]) for piece in cuts(ref.at[n])]
        rows, lanes = ref.shape
        most = max(16, CUT // (lanes * 2) // 16 * 16)
        count = -(-rows // most)
        size = -(-rows // count // 16) * 16
        return [ref.at[pl.ds(n, min(size, rows - n)), :] for n in range(0, rows, size)]

    def copies(src, dst, send_at, recv_at, device):
        return [
            pltpu.make_async_remote_copy(
                src_ref=one,
                dst_ref=other_,
                send_sem=send_sems.at[send_at],
                recv_sem=recv_sems.at[recv_at],
                device_id=device,
                device_id_type=MESH,
            )
            for one, other_ in zip(cuts(src), cuts(dst))
        ]

    def send(src, dst, group, key, device):
        size = size_of(src)
        for copy in copies(src, dst, send_no.add(group, size), recv_no.add(key, size), device):
            copy.start()

    def send_unless(own, src, dst, group, device, recv_at):
        @pl.when(own)
        def _():
            pltpu.make_async_copy(src, dst, recv_sems.at[recv_at]).start()

        @pl.when(jnp.logical_not(own))
        def _():
            for copy in copies(src, dst, send_no(group), recv_at, device):
                copy.start()

    def recv(key):
        dummy(recv_no.bytes[key], recv_at=recv_no(key)).wait_recv()

    def w_rows(a, yy, zz):
        return W.at[a, yy, pl.ds(pl.multiple_of(zz * 192, 192), 192), :]

    w_base = recv_no("w", 4)

    def w_out(a, h):
        zt = 2 * k + h
        send_unless(
            jnp.logical_and(zt == zh, k == a),
            (wu, wd)[a].at[:, h * 384 : (h + 1) * 384],
            w_rows(a, y, zh),
            "w",
            dev(zz=2 * zt + zl, core=a),
            w_base + zh,
        )

    for a, src in enumerate((tok, og)):
        send(src.at[:, other], part(a, k), "half", "half", sib)

    def lanes_of(zz):
        return pl.ds(pl.multiple_of(lax.div(zz, 2) * 128, 128), 128)

    def tok_shard(xx, zz):
        start = lax.rem(zz, 2) * 384
        return X.at[0, xx, pl.ds(pl.multiple_of(start, 384), 384), lanes_of(zz)]

    def og_shard(xx, zz):
        start = lax.rem(zz, 2) * 384
        return X.at[1, xx, pl.ds(pl.multiple_of(start, 384), 192), lanes_of(zz)]

    def rest_shard(xx, start, size):
        first = zl * 384 + 192 + start
        return X.at[1, xx, pl.ds(pl.multiple_of(first, 96), size), lanes_of(z)]

    def rest_shards(xs, zz):
        first = lax.rem(zz, 2) * 384 + 192
        return X.at[1, xs, pl.ds(pl.multiple_of(first, 192), 192), lanes_of(zz)]

    steps = [[0], [-1, 1], [-2, 2], [-3, 3], [4]]

    def near(rel, n, block):
        send(block, block, "x", ("x", -1, rel) if n == rel % 2 else "near", xp)
        send(block, block, "x", ("x", 1, rel) if n != rel % 2 else "near", xm)

    def first():
        block = part(0, k)
        for device, key in ((xp, -1), (xm, 1)):
            send(tok.at[:, mine], block, "x", ("x", key, 0) if key == -1 else "near", device)
        send(tok.at[:, mine], block, "z", ("z", -1, 0), zp)
        send(tok.at[:, mine], block, "z", ("z", 1, 0), zm)

    def arrive(step):
        for rel in steps[step]:
            blocks = [tok_shard(x, mod8(z + rel)), og_shard(x, mod8(z + rel))]
            if step == 0:
                blocks[0] = part(0, o)
            for n, block in enumerate(blocks):
                if step > 0:
                    recv(("z", rel, n))
                if step < 3 and rel <= 0:
                    send(block, block, "z", ("z", rel - 1, n), zp)
                if step < 3 and rel >= 0:
                    send(block, block, "z", ("z", rel + 1, n), zm)
                if rel == -3 and n == 0:
                    send(block, block, "z", ("z", 4, n), zp)
                if rel == 3 and n == 1:
                    send(block, block, "z", ("z", 4, n), zm)
            for n, block in enumerate(blocks):
                near(rel, n, block)

    def across(step):
        for rel in steps[step]:
            zz = mod8(z + rel)
            shards = (tok_shard, og_shard) if rel % 2 == 0 else (og_shard, tok_shard)
            left, right = shards[0](mod4(x - 1), zz), shards[1](mod4(x + 1), zz)
            recv(("x", -1, rel))
            send(left, left, "x", "far", xp)
            recv(("x", 1, rel))
            send(right, right, "x", "far", xm)

    def rest_x(step):
        if step == 0:
            block = rest_shard(x, 0, 192)
            send(block, block, "rest x", "rest near", xp)
            send(block, block, "rest x", "rest near", xm)
        if step == 1:
            recv("rest near")
            left, right = rest_shard(mod4(x - 1), 0, 96), rest_shard(mod4(x + 1), 96, 96)
            send(left, left, "rest x", "rest far", xp)
            send(right, right, "rest x", "rest far", xm)
        if step == 2:
            recv("rest far")

    def rest_z(step):
        for way in (-1, 1):
            if step > 0:
                recv(("rest", way * step))
            if step < 3:
                block = rest_shards(slice(0, 4), mod8(z + way * step))
                send(block, block, "rest", ("rest", way * (step + 1)), zp if way < 0 else zm)
            else:
                xs = slice(0, 2) if way < 0 else slice(2, 4)
                block = rest_shards(xs, mod8(z + way * step))
                send(block, block, "rest", ("rest", 4), zp if way < 0 else zm)

    order = [0, 1, 3, 2]

    def w_in(i):
        zz = mod4(zh + order[i])
        block = w_rows(k, y, zz)
        dummy(BLOCK, recv_at=w_base + zz).wait_recv()
        send(block, block, "wy", ("wy", -1, i), yp)
        send(block, block, "wy", ("wy", 1, i), ym)
        send(block, block, "wk", "wk", sib)

    def w_ring(i):
        zz = mod4(zh + order[i])
        left, right = w_rows(k, mod4(y - 1), zz), w_rows(k, mod4(y + 1), zz)
        recv(("wy", -1, i))
        if i % 2 == 0:
            send(left, left, "wy", "wy far", yp)
        send(left, left, "wk", "wk", sib)
        recv(("wy", 1, i))
        if i % 2 == 1:
            send(right, right, "wy", "wy far", ym)
        send(right, right, "wk", "wk", sib)

    first()
    w_out(0, 0)
    for a in range(2):
        kept[a].wait()
    recv("half")
    arrive(0)
    rest_x(0)
    w_out(0, 1)
    arrive(1)
    rest_x(1)
    w_out(1, 0)
    w_out(1, 1)
    w_in(0)
    across(0)
    w_in(1)
    w_in(2)
    arrive(2)
    w_in(3)
    rest_x(2)
    rest_z(0)
    across(1)
    w_ring(0)
    arrive(3)
    w_ring(1)
    rest_z(1)
    w_ring(2)
    arrive(4)
    rest_z(2)
    across(2)
    w_ring(3)
    rest_z(3)
    across(3)
    recv("wy far")
    far = W.at[k, mod4(y + 2)]
    send(far, far, "wk", "wk", sib)
    across(4)
    recv("wk")

    def hidden_term(a, rel):
        blk = mod4(x + rel)
        term = lax.dot_general(
            W[a, blk], X[a, blk], (((0,), (0,)), ((), ())), preferred_element_type=F32
        )
        if rel == 0:
            H[a] = term
        else:
            H[a] += term

    recv("near")
    for rel in (0, -1, 1):
        hidden_term(0, rel)
    recv(("rest", 4))
    for rel in (0, -1, 1):
        hidden_term(1, rel)
    recv("far")
    for a in range(2):
        hidden_term(a, 2)

    @pl.loop(0, 6)
    def _(i):
        rows = pl.ds(pl.multiple_of(i * 64, 64), 64)
        active, slope = gelu_pair(H[0, rows, :])
        hb[0, rows, :] = (H[1, rows, :] * slope).astype(BF16)
        hb[1, rows, :] = active.astype(BF16)

    def rows_of(start, size, align):
        return pl.ds(pl.multiple_of(start, align), size)

    def ig_block(rel):
        for i in range(3):
            rows = slice(i * 256, (i + 1) * 256)
            value = jnp.dot(W[0, mod4(x + rel), rows, :], hb[0], preferred_element_type=F32)
            if rel != 0:
                igb[rel % 4, rows, :] = value.astype(BF16)
            if rel != 2:
                igf[rel % 4, rows, :] = value

    def ig_spot(g, t):
        zt = mod8(z + (4 - g) * (1, -1)[t])
        whole = 0 < g < 4
        start = lax.rem(zt, 2) * 384 + (0 if whole else 192 * t)
        rows = rows_of(start, 384 if whole else 192, 192)
        return rows, rows_of(lax.div(zt, 2) * 128, 128, 128)

    def height(g):
        return slice(0, 384 if 0 < g < 4 else 192)

    def ig_s1(g):
        for t in range(2):
            send(
                igb.at[(2, *ig_spot(g, t))], igr.at[0, g, t, height(g)],
                "ig", ("ig", 0, g), (xp, xm)[t],
            )

    def ig_s2(g):
        for t in range(2):
            send(
                igb.at[((3, 1)[t], *ig_spot(g, t))], igr.at[1, g, t, height(g)],
                "ig", ("ig", 1, g), (xm, xp)[t],
            )

    def ig_got(stage, g, t):
        return igr[stage, g, t, height(g), :].astype(F32)

    def ig_s3(g):
        recv(("ig", 0, g))
        for t in range(2):
            value = igf[((1, 3)[t], *ig_spot(g, t))] + ig_got(0, g, t)
            igs[g, t, height(g), :] = value.astype(BF16)
            send(
                igs.at[g, t, height(g)], igr.at[2, g, t, height(g)],
                "ig", ("ig", 1, g), (xp, xm)[t],
            )

    def zc_got(g, t):
        return zr[g, t, height(g), :].astype(F32)

    def ig_s4(g):
        recv(("ig", 1, g))
        if 0 < g < 4:
            recv(("zc", g - 1))
        for t in range(2):
            value = igf[(0, *ig_spot(g, t))] + ig_got(1, g, t) + ig_got(2, g, t)
            if g == 4:
                own_sum[192 * t : 192 * (t + 1), :] = value
                continue
            if g > 1:
                value = value + zc_got(g - 1, t)
            zs[g, t, height(g), :] = value.astype(BF16)
            if g == 1:
                part_rows = slice(192 * t, 192 * (t + 1))
                summed = value[part_rows] + zc_got(0, t)
                zs[g, t, part_rows, :] = summed.astype(BF16)
            send(
                zs.at[g, t, height(g)], zr.at[g, t, height(g)],
                "zc", ("zc", g), (zp, zm)[t],
            )

    def dw_block(a, rel, rows):
        return lax.dot_general(
            X[a, mod4(y + rel), rows, :], hb[a], (((1,), (1,)), ((), ())),
            preferred_element_type=F32,
        )

    def dw_other(rel):
        for i in range(2):
            rows = slice(i * 384, (i + 1) * 384)
            ds[rel % 4, rows, :] = dw_block(o, rel, rows).astype(BF16)
            send(ds.at[rel % 4, rows, :], dr.at[rel % 4, rows, :], "dk", ("dk", rel), sib)

    def dw_own(rel):
        for i in range(2):
            rows = slice(i * 384, (i + 1) * 384)
            df[rel % 4, rows, :] = dw_block(k, rel, rows)

    def dw_sum(rel):
        recv(("dk", rel))

    def dw_value(rel, q, t):
        rows = slice(384 * t + 96 * q, 384 * t + 96 * (q + 1))
        return df[rel % 4, rows, :] + dr[rel % 4, rows, :].astype(F32)

    def dw_send(stage, q, t, value, device):
        dws[stage, q, t] = value.astype(BF16)
        send(dws.at[stage, q, t], dwr.at[stage, q, t], "dw", ("dw", min(stage, 1), q), device)

    def dw_got(stage, q, t):
        return dwr[stage, q, t].astype(F32)

    def dw_s1(q):
        for t in range(2):
            dw_send(0, q, t, dw_value(2, q, t), (yp, ym)[t])

    def dw_s2(q):
        for t in range(2):
            dw_send(1, q, t, dw_value((-1, 1)[t], q, t), (ym, yp)[t])

    def dw_s3(q):
        recv(("dw", 0, q))
        for t in range(2):
            dw_send(2, q, t, dw_value((1, -1)[t], q, t) + dw_got(0, q, t), (yp, ym)[t])

    d_at = recv_no("dl")

    def dw_place(a, h, q):
        start = pl.multiple_of(a * 768 + h * 384, 384)
        return dw_out.at[96 * (q % 2) : 96 * (q % 2 + 1), pl.ds(start, 384)]

    def dw_s4(q):
        recv(("dw", 1, q))
        for t in range(2):
            value = dw_value(0, q, t) + dw_got(1, q, t) + dw_got(2, q, t)
            dwl[q, t] = value.astype(BF16)
            zf = 2 * t + q // 2
            half = lax.rem(zh, 2)
            send_unless(
                jnp.logical_and(zf == zh, lax.div(zh, 2) == k),
                dwl.at[q, t],
                dw_place(k, half, q),
                "dl",
                dev(zz=2 * zf + zl, core=lax.div(zh, 2)),
                d_at,
            )

    dw_other(2)
    ig_block(2)
    ig_s1(0)
    dw_own(2)
    ig_block(1)
    ig_block(-1)
    ig_s2(0)
    ig_s1(1)
    dw_sum(2)
    dw_s1(0)
    dw_s1(1)
    dw_other(1)
    dw_other(-1)
    dw_other(0)
    dw_own(1)
    dw_own(-1)
    dw_own(0)
    ig_s3(0)
    ig_s2(1)
    ig_block(0)
    dw_sum(1)
    dw_sum(-1)
    dw_s2(0)
    dw_sum(0)
    ig_s1(2)
    dw_s3(0)
    dw_s2(1)
    ig_s3(1)
    ig_s2(2)
    ig_s4(0)
    dw_s1(2)
    ig_s1(3)
    dw_s3(1)
    dw_s2(2)
    dw_s4(0)
    ig_s3(2)
    ig_s2(3)
    ig_s4(1)
    dw_s1(3)
    ig_s1(4)
    dw_s3(2)
    dw_s2(3)
    dw_s4(1)
    ig_s3(3)
    ig_s2(4)
    ig_s4(2)
    dw_s3(3)
    dw_s4(2)
    ig_s3(4)
    ig_s4(3)
    ig_s4(4)
    dw_s4(3)

    recv(("zc", 3))
    last[...] = (own_sum[...] + zc_got(3, 0) + zc_got(3, 1)).astype(BF16)
    half = lambda core: last.at[pl.ds(pl.multiple_of(core * 192, 192), 192), :]
    send(half(o), ig_out.at[:, mine], "last", "last", sib)
    copy = pltpu.make_async_copy(half(k), ig_out.at[:, mine], local_sems.at[2])
    copy.start()
    copy.wait()
    recv("last")
    dummy(8 * BLOCK // 2, recv_at=d_at).wait_recv()

    for group, size in send_no.bytes.items():
        dummy(size, send_at=send_no(group)).wait_send()
    some_own = lax.div(zh, 2) == k

    @pl.when(some_own)
    def _():
        dummy(3 * BLOCK, send_at=send_no("w")).wait_send()
        dummy(6 * BLOCK // 2, send_at=send_no("dl")).wait_send()

    @pl.when(jnp.logical_not(some_own))
    def _():
        dummy(4 * BLOCK, send_at=send_no("w")).wait_send()
        dummy(8 * BLOCK // 2, send_at=send_no("dl")).wait_send()

    assert send_no.count <= SENDS and recv_no.count <= RECVS


def body(tokens, out_grad, w_up, w_down):
    any_ = pl.BlockSpec(memory_space=pl.ANY)
    dw, ig = pl.pallas_call(
        kernel,
        out_shape=(
            jax.ShapeDtypeStruct((192, 1536), BF16),
            jax.ShapeDtypeStruct((192, 256), BF16),
        ),
        in_specs=[any_] * 4,
        out_specs=(any_, any_),
        scratch_shapes=[
            pltpu.VMEM((2, 4, 768, 512), BF16),
            pltpu.VMEM((2, 4, 768, 384), BF16),
            pltpu.VMEM((2, 384, 512), F32),
            pltpu.VMEM((2, 384, 512), BF16),
            pltpu.VMEM((4, 768, 512), BF16),
            pltpu.VMEM((4, 768, 512), F32),
            pltpu.VMEM((5, 2, 384, 128), BF16),
            pltpu.VMEM((3, 5, 2, 384, 128), BF16),
            pltpu.VMEM((4, 2, 384, 128), BF16),
            pltpu.VMEM((4, 2, 384, 128), BF16),
            pltpu.VMEM((384, 128), F32),
            pltpu.VMEM((384, 128), BF16),
            pltpu.VMEM((4, 768, 384), BF16),
            pltpu.VMEM((4, 768, 384), BF16),
            pltpu.VMEM((4, 768, 384), F32),
            pltpu.VMEM((3, 4, 2, 96, 384), BF16),
            pltpu.VMEM((3, 4, 2, 96, 384), BF16),
            pltpu.VMEM((4, 2, 96, 384), BF16),
            pltpu.SemaphoreType.DMA((SENDS,)),
            pltpu.SemaphoreType.DMA((RECVS,)),
            pltpu.SemaphoreType.DMA((4,)),
        ],
        compiler_params=pltpu.CompilerParams(
            collective_id=0, has_side_effects=True, vmem_limit_bytes=58 * 2**20
        ),
        cost_estimate=pl.CostEstimate(
            flops=6 * 10**9, bytes_accessed=4 * 10**6, transcendentals=2 * 10**5
        ),
        name="ffn_backward",
    )(tokens.T, out_grad.T, w_up, w_down)
    factor = 1.0 / math.sqrt(tokens.shape[0] * lax.axis_size("row"))
    return (ig.T, dw[:, :768].astype(F32) * factor, dw[:, 768:].astype(F32) * factor)


def solution(mesh):
    return jax.shard_map(
        body,
        mesh=mesh,
        in_specs=(P("row", "col"), P("row", "col"), P("row", "col"), P("row", "col")),
        out_specs=(P("row", "col"), P("row", "col"), P("row", "col")),
        check_vma=False,
    )
```

```python
import math

import jax
import jax.numpy as jnp
from jax import lax
from jax.experimental import pallas as pl
from jax.experimental.pallas import tpu as pltpu
from jax.sharding import PartitionSpec as P

gelu_coef = math.sqrt(2.0 / math.pi)
cubic_coef = 0.044715
MESH = pl.DeviceIdType.MESH
BF16 = jnp.bfloat16
F32 = jnp.float32


def gelu_pair(hidden):
    inner = gelu_coef * (hidden + cubic_coef * hidden * hidden * hidden)
    tangent = jnp.tanh(inner)
    active = 0.5 * hidden * (1.0 + tangent)
    slope = 0.5 * (1.0 + tangent) + 0.5 * hidden * (1.0 - tangent * tangent) * gelu_coef * (
        1.0 + 3.0 * cubic_coef * hidden * hidden
    )
    return (active, slope)


class Slots:
    def __init__(self):
        self.at = {}
        self.count = 0
        self.bytes = {}

    def __call__(self, key, extent=1):
        if key not in self.at:
            self.at[key] = self.count
            self.count += extent
        return self.at[key]

    def add(self, key, size):
        self.bytes[key] = self.bytes.get(key, 0) + size
        return self(key)


SENDS = 14
RECVS = 86
BLOCK = 192 * 384 * 2
CUT = 98304


def kernel(
    tok, og, wu, wd, dw_out, ig_out,
    X, W, H, hb, igb, igf, igs, igr, zs, zr, own_sum, last, ds, dr, df, dws, dwr, dwl,
    send_sems, recv_sems, local_sems,
):
    row, col = lax.axis_index("row"), lax.axis_index("col")
    x, y = lax.div(col, 4), lax.div(row, 4)
    zh, zl, k = lax.rem(row, 4), lax.rem(lax.div(col, 2), 2), lax.rem(col, 2)
    z = 2 * zh + zl
    o = 1 - k
    mod4 = lambda v: lax.rem(v + 8, 4)
    mod8 = lambda v: lax.rem(v + 16, 8)

    def dev(dx=0, dy=0, zz=None, core=None):
        zz = z if zz is None else zz
        core = k if core is None else core
        xx = mod4(x + dx) if dx else x
        yy = mod4(y + dy) if dy else y
        return (yy * 4 + lax.div(zz, 2), xx * 4 + lax.rem(zz, 2) * 2 + core)

    sib = dev(core=o)
    xp, xm = dev(dx=1), dev(dx=-1)
    yp, ym = dev(dy=1), dev(dy=-1)
    zp, zm = dev(zz=mod8(z + 1)), dev(zz=mod8(z - 1))

    def part(a, core):
        return X.at[
            a, x,
            pl.ds(pl.multiple_of(zl * 384 + core * 192, 192), 192),
            pl.ds(pl.multiple_of(zh * 128, 128), 128),
        ]

    mine = pl.ds(pl.multiple_of(k * 128, 128), 128)
    other = pl.ds(pl.multiple_of(o * 128, 128), 128)
    kept = [
        pltpu.make_async_copy(src.at[:, mine], part(a, k), local_sems.at[a])
        for a, src in enumerate((tok, og))
    ]
    for copy in kept:
        copy.start()

    barrier = pltpu.get_barrier_semaphore()
    partners = [dev(zz=mod8(z + rel), core=core) for rel in (4, 2, 6) for core in (k, o)]
    partners += [xp, xm, yp, ym, zp, zm, sib]
    for partner in partners:
        pl.semaphore_signal(barrier, inc=1, device_id=partner, device_id_type=MESH)
    pl.semaphore_wait(barrier, len(partners))

    send_no, recv_no = Slots(), Slots()

    def size_of(ref):
        return math.prod(ref.shape) * 2

    def view(size):
        for lanes in (512, 384, 256, 128):
            for lead in (1, 2, 3, 4, 6, 8):
                rows, rest = divmod(size, lead * lanes * 2)
                if rest == 0 and rows <= 768 and rows % 16 == 0:
                    if lead < 5:
                        return X.at[0, :lead, :rows, :lanes]
                    return X.at[:, : lead // 2, :rows, :lanes]
        raise ValueError(size)

    def dummy(size, send_at=0, recv_at=0):
        return pltpu.make_async_remote_copy(
            src_ref=view(size),
            dst_ref=view(size),
            send_sem=send_sems.at[send_at],
            recv_sem=recv_sems.at[recv_at],
            device_id=sib,
            device_id_type=MESH,
        )

    def cuts(ref):
        if len(ref.shape) == 3:
            return [piece for n in range(ref.shape[0]) for piece in cuts(ref.at[n])]
        rows, lanes = ref.shape
        most = max(16, CUT // (lanes * 2) // 16 * 16)
        count = -(-rows // most)
        size = -(-rows // count // 16) * 16
        return [ref.at[pl.ds(n, min(size, rows - n)), :] for n in range(0, rows, size)]

    def copies(src, dst, send_at, recv_at, device):
        return [
            pltpu.make_async_remote_copy(
                src_ref=one,
                dst_ref=other_,
                send_sem=send_sems.at[send_at],
                recv_sem=recv_sems.at[recv_at],
                device_id=device,
                device_id_type=MESH,
            )
            for one, other_ in zip(cuts(src), cuts(dst))
        ]

    def send(src, dst, group, key, device):
        size = size_of(src)
        for copy in copies(src, dst, send_no.add(group, size), recv_no.add(key, size), device):
            copy.start()

    def send_unless(own, src, dst, group, device, recv_at):
        @pl.when(own)
        def _():
            pltpu.make_async_copy(src, dst, recv_sems.at[recv_at]).start()

        @pl.when(jnp.logical_not(own))
        def _():
            for copy in copies(src, dst, send_no(group), recv_at, device):
                copy.start()

    def recv(key):
        dummy(recv_no.bytes[key], recv_at=recv_no(key)).wait_recv()

    def w_rows(a, yy, zz):
        return W.at[a, yy, pl.ds(pl.multiple_of(zz * 192, 192), 192), :]

    w_base = recv_no("w", 4)

    def w_out(a, h):
        zt = 2 * k + h
        send_unless(
            jnp.logical_and(zt == zh, k == a),
            (wu, wd)[a].at[:, h * 384 : (h + 1) * 384],
            w_rows(a, y, zh),
            "w",
            dev(zz=2 * zt + zl, core=a),
            w_base + zh,
        )

    for a, src in enumerate((tok, og)):
        send(src.at[:, other], part(a, k), "half", "half", sib)

    def lanes_of(zz):
        return pl.ds(pl.multiple_of(lax.div(zz, 2) * 128, 128), 128)

    def tok_shard(xx, zz):
        start = lax.rem(zz, 2) * 384
        return X.at[0, xx, pl.ds(pl.multiple_of(start, 384), 384), lanes_of(zz)]

    def og_shard(xx, zz):
        start = lax.rem(zz, 2) * 384
        return X.at[1, xx, pl.ds(pl.multiple_of(start, 384), 192), lanes_of(zz)]

    def rest_shard(xx, start, size):
        first = zl * 384 + 192 + start
        return X.at[1, xx, pl.ds(pl.multiple_of(first, 96), size), lanes_of(z)]

    def rest_shards(xs, zz):
        first = lax.rem(zz, 2) * 384 + 192
        return X.at[1, xs, pl.ds(pl.multiple_of(first, 192), 192), lanes_of(zz)]

    steps = [[0], [-1, 1], [-2, 2], [-3, 3], [4]]

    def near(rel, n, block):
        send(block, block, "x", ("x", -1, rel) if n == rel % 2 else "near", xp)
        send(block, block, "x", ("x", 1, rel) if n != rel % 2 else "near", xm)

    def first():
        block = part(0, k)
        for device, key in ((xp, -1), (xm, 1)):
            send(tok.at[:, mine], block, "x", ("x", key, 0) if key == -1 else "near", device)
        send(tok.at[:, mine], block, "z", ("z", -1, 0), zp)
        send(tok.at[:, mine], block, "z", ("z", 1, 0), zm)

    def arrive(step):
        for rel in steps[step]:
            blocks = [tok_shard(x, mod8(z + rel)), og_shard(x, mod8(z + rel))]
            if step == 0:
                blocks[0] = part(0, o)
            for n, block in enumerate(blocks):
                if step > 0:
                    recv(("z", rel, n))
                if step < 3 and rel <= 0:
                    send(block, block, "z", ("z", rel - 1, n), zp)
                if step < 3 and rel >= 0:
                    send(block, block, "z", ("z", rel + 1, n), zm)
                if rel == -3 and n == 0:
                    send(block, block, "z", ("z", 4, n), zp)
                if rel == 3 and n == 1:
                    send(block, block, "z", ("z", 4, n), zm)
            for n, block in enumerate(blocks):
                near(rel, n, block)

    def across(step):
        for rel in steps[step]:
            zz = mod8(z + rel)
            shards = (tok_shard, og_shard) if rel % 2 == 0 else (og_shard, tok_shard)
            left, right = shards[0](mod4(x - 1), zz), shards[1](mod4(x + 1), zz)
            recv(("x", -1, rel))
            send(left, left, "x", "far", xp)
            recv(("x", 1, rel))
            send(right, right, "x", "far", xm)

    def rest_x(step):
        if step == 0:
            block = rest_shard(x, 0, 192)
            send(block, block, "rest x", "rest near", xp)
            send(block, block, "rest x", "rest near", xm)
        if step == 1:
            recv("rest near")
            left, right = rest_shard(mod4(x - 1), 0, 96), rest_shard(mod4(x + 1), 96, 96)
            send(left, left, "rest x", "rest far", xp)
            send(right, right, "rest x", "rest far", xm)
        if step == 2:
            recv("rest far")

    def rest_z(step):
        for way in (-1, 1):
            if step > 0:
                recv(("rest", way * step))
            if step < 3:
                block = rest_shards(slice(0, 4), mod8(z + way * step))
                send(block, block, "rest", ("rest", way * (step + 1)), zp if way < 0 else zm)
            else:
                xs = slice(0, 2) if way < 0 else slice(2, 4)
                block = rest_shards(xs, mod8(z + way * step))
                send(block, block, "rest", ("rest", 4), zp if way < 0 else zm)

    order = [0, 1, 3, 2]

    def w_in(i):
        zz = mod4(zh + order[i])
        block = w_rows(k, y, zz)
        dummy(BLOCK, recv_at=w_base + zz).wait_recv()
        send(block, block, "wy", ("wy", -1, i), yp)
        send(block, block, "wy", ("wy", 1, i), ym)
        send(block, block, "wk", "wk", sib)

    def w_ring(i):
        zz = mod4(zh + order[i])
        left, right = w_rows(k, mod4(y - 1), zz), w_rows(k, mod4(y + 1), zz)
        recv(("wy", -1, i))
        if i % 2 == 0:
            send(left, left, "wy", "wy far", yp)
        send(left, left, "wk", "wk", sib)
        recv(("wy", 1, i))
        if i % 2 == 1:
            send(right, right, "wy", "wy far", ym)
        send(right, right, "wk", "wk", sib)

    first()
    w_out(0, 0)
    for a in range(2):
        kept[a].wait()
    recv("half")
    rest_x(0)
    arrive(0)
    w_out(0, 1)
    arrive(1)
    w_out(1, 0)
    w_out(1, 1)
    rest_x(1)
    w_in(0)
    across(0)
    w_in(1)
    w_in(2)
    arrive(2)
    w_in(3)
    rest_x(2)
    rest_z(0)
    across(1)
    w_ring(0)
    arrive(3)
    w_ring(1)
    rest_z(1)
    w_ring(2)
    arrive(4)
    rest_z(2)
    across(2)
    w_ring(3)
    rest_z(3)
    across(3)
    recv("wy far")
    far = W.at[k, mod4(y + 2)]
    send(far, far, "wk", "wk", sib)
    across(4)
    recv("wk")

    def hidden_term(a, rel):
        blk = mod4(x + rel)
        term = lax.dot_general(
            W[a, blk], X[a, blk], (((0,), (0,)), ((), ())), preferred_element_type=F32
        )
        if rel == 0:
            H[a] = term
        else:
            H[a] += term

    recv("near")
    for rel in (0, -1, 1):
        hidden_term(0, rel)
    recv(("rest", 4))
    for rel in (0, -1, 1):
        hidden_term(1, rel)
    recv("far")
    for a in range(2):
        hidden_term(a, 2)

    @pl.loop(0, 6)
    def _(i):
        rows = pl.ds(pl.multiple_of(i * 64, 64), 64)
        active, slope = gelu_pair(H[0, rows, :])
        hb[0, rows, :] = (H[1, rows, :] * slope).astype(BF16)
        hb[1, rows, :] = active.astype(BF16)

    def rows_of(start, size, align):
        return pl.ds(pl.multiple_of(start, align), size)

    def ig_block(rel):
        for i in range(3):
            rows = slice(i * 256, (i + 1) * 256)
            value = jnp.dot(W[0, mod4(x + rel), rows, :], hb[0], preferred_element_type=F32)
            if rel != 0:
                igb[rel % 4, rows, :] = value.astype(BF16)
            if rel != 2:
                igf[rel % 4, rows, :] = value

    def ig_spot(g, t):
        zt = mod8(z + (4 - g) * (1, -1)[t])
        whole = 0 < g < 4
        start = lax.rem(zt, 2) * 384 + (0 if whole else 192 * t)
        rows = rows_of(start, 384 if whole else 192, 192)
        return rows, rows_of(lax.div(zt, 2) * 128, 128, 128)

    def height(g):
        return slice(0, 384 if 0 < g < 4 else 192)

    def ig_s1(g):
        for t in range(2):
            send(
                igb.at[(2, *ig_spot(g, t))], igr.at[0, g, t, height(g)],
                "ig", ("ig", 0, g), (xp, xm)[t],
            )

    def ig_s2(g):
        for t in range(2):
            send(
                igb.at[((3, 1)[t], *ig_spot(g, t))], igr.at[1, g, t, height(g)],
                "ig", ("ig", 1, g), (xm, xp)[t],
            )

    def ig_got(stage, g, t):
        return igr[stage, g, t, height(g), :].astype(F32)

    def ig_s3(g):
        recv(("ig", 0, g))
        for t in range(2):
            value = igf[((1, 3)[t], *ig_spot(g, t))] + ig_got(0, g, t)
            igs[g, t, height(g), :] = value.astype(BF16)
            send(
                igs.at[g, t, height(g)], igr.at[2, g, t, height(g)],
                "ig", ("ig", 1, g), (xp, xm)[t],
            )

    def zc_got(g, t):
        return zr[g, t, height(g), :].astype(F32)

    def ig_s4(g):
        recv(("ig", 1, g))
        if 0 < g < 4:
            recv(("zc", g - 1))
        for t in range(2):
            value = igf[(0, *ig_spot(g, t))] + ig_got(1, g, t) + ig_got(2, g, t)
            if g == 4:
                own_sum[192 * t : 192 * (t + 1), :] = value
                continue
            if g > 1:
                value = value + zc_got(g - 1, t)
            zs[g, t, height(g), :] = value.astype(BF16)
            if g == 1:
                part_rows = slice(192 * t, 192 * (t + 1))
                summed = value[part_rows] + zc_got(0, t)
                zs[g, t, part_rows, :] = summed.astype(BF16)
            send(
                zs.at[g, t, height(g)], zr.at[g, t, height(g)],
                "zc", ("zc", g), (zp, zm)[t],
            )

    def dw_block(a, rel, rows):
        return lax.dot_general(
            X[a, mod4(y + rel), rows, :], hb[a], (((1,), (1,)), ((), ())),
            preferred_element_type=F32,
        )

    def dw_other(rel):
        for i in range(2):
            rows = slice(i * 384, (i + 1) * 384)
            ds[rel % 4, rows, :] = dw_block(o, rel, rows).astype(BF16)
            send(ds.at[rel % 4, rows, :], dr.at[rel % 4, rows, :], "dk", ("dk", rel), sib)

    def dw_own(rel):
        for i in range(2):
            rows = slice(i * 384, (i + 1) * 384)
            df[rel % 4, rows, :] = dw_block(k, rel, rows)

    def dw_sum(rel):
        recv(("dk", rel))

    def dw_value(rel, q, t):
        rows = slice(384 * t + 96 * q, 384 * t + 96 * (q + 1))
        return df[rel % 4, rows, :] + dr[rel % 4, rows, :].astype(F32)

    def dw_send(stage, q, t, value, device):
        dws[stage, q, t] = value.astype(BF16)
        send(dws.at[stage, q, t], dwr.at[stage, q, t], "dw", ("dw", min(stage, 1), q), device)

    def dw_got(stage, q, t):
        return dwr[stage, q, t].astype(F32)

    def dw_s1(q):
        for t in range(2):
            dw_send(0, q, t, dw_value(2, q, t), (yp, ym)[t])

    def dw_s2(q):
        for t in range(2):
            dw_send(1, q, t, dw_value((-1, 1)[t], q, t), (ym, yp)[t])

    def dw_s3(q):
        recv(("dw", 0, q))
        for t in range(2):
            dw_send(2, q, t, dw_value((1, -1)[t], q, t) + dw_got(0, q, t), (yp, ym)[t])

    d_at = recv_no("dl")

    def dw_place(a, h, q):
        start = pl.multiple_of(a * 768 + h * 384, 384)
        return dw_out.at[96 * (q % 2) : 96 * (q % 2 + 1), pl.ds(start, 384)]

    def dw_s4(q):
        recv(("dw", 1, q))
        for t in range(2):
            value = dw_value(0, q, t) + dw_got(1, q, t) + dw_got(2, q, t)
            dwl[q, t] = value.astype(BF16)
            zf = 2 * t + q // 2
            half = lax.rem(zh, 2)
            send_unless(
                jnp.logical_and(zf == zh, lax.div(zh, 2) == k),
                dwl.at[q, t],
                dw_place(k, half, q),
                "dl",
                dev(zz=2 * zf + zl, core=lax.div(zh, 2)),
                d_at,
            )

    dw_other(2)
    ig_block(2)
    ig_s1(0)
    dw_own(2)
    ig_block(1)
    ig_block(-1)
    ig_s2(0)
    ig_s1(1)
    dw_sum(2)
    dw_s1(0)
    dw_s1(1)
    dw_other(1)
    dw_other(-1)
    dw_other(0)
    dw_own(1)
    dw_own(-1)
    dw_own(0)
    ig_s3(0)
    ig_s2(1)
    ig_block(0)
    dw_sum(1)
    dw_sum(-1)
    dw_s2(0)
    dw_sum(0)
    ig_s1(2)
    dw_s3(0)
    dw_s2(1)
    ig_s3(1)
    ig_s2(2)
    ig_s4(0)
    dw_s1(2)
    ig_s1(3)
    dw_s3(1)
    dw_s2(2)
    dw_s4(0)
    ig_s3(2)
    ig_s2(3)
    ig_s4(1)
    dw_s1(3)
    ig_s1(4)
    dw_s3(2)
    dw_s2(3)
    dw_s4(1)
    ig_s3(3)
    ig_s2(4)
    ig_s4(2)
    dw_s3(3)
    dw_s4(2)
    ig_s3(4)
    ig_s4(3)
    ig_s4(4)
    dw_s4(3)

    recv(("zc", 3))
    last[...] = (own_sum[...] + zc_got(3, 0) + zc_got(3, 1)).astype(BF16)
    half = lambda core: last.at[pl.ds(pl.multiple_of(core * 192, 192), 192), :]
    send(half(o), ig_out.at[:, mine], "last", "last", sib)
    copy = pltpu.make_async_copy(half(k), ig_out.at[:, mine], local_sems.at[2])
    copy.start()
    copy.wait()
    recv("last")
    dummy(8 * BLOCK // 2, recv_at=d_at).wait_recv()

    for group, size in send_no.bytes.items():
        dummy(size, send_at=send_no(group)).wait_send()
    some_own = lax.div(zh, 2) == k

    @pl.when(some_own)
    def _():
        dummy(3 * BLOCK, send_at=send_no("w")).wait_send()
        dummy(6 * BLOCK // 2, send_at=send_no("dl")).wait_send()

    @pl.when(jnp.logical_not(some_own))
    def _():
        dummy(4 * BLOCK, send_at=send_no("w")).wait_send()
        dummy(8 * BLOCK // 2, send_at=send_no("dl")).wait_send()

    assert send_no.count <= SENDS and recv_no.count <= RECVS


def body(tokens, out_grad, w_up, w_down):
    any_ = pl.BlockSpec(memory_space=pl.ANY)
    dw, ig = pl.pallas_call(
        kernel,
        out_shape=(
            jax.ShapeDtypeStruct((192, 1536), BF16),
            jax.ShapeDtypeStruct((192, 256), BF16),
        ),
        in_specs=[any_] * 4,
        out_specs=(any_, any_),
        scratch_shapes=[
            pltpu.VMEM((2, 4, 768, 512), BF16),
            pltpu.VMEM((2, 4, 768, 384), BF16),
            pltpu.VMEM((2, 384, 512), F32),
            pltpu.VMEM((2, 384, 512), BF16),
            pltpu.VMEM((4, 768, 512), BF16),
            pltpu.VMEM((4, 768, 512), F32),
            pltpu.VMEM((5, 2, 384, 128), BF16),
            pltpu.VMEM((3, 5, 2, 384, 128), BF16),
            pltpu.VMEM((4, 2, 384, 128), BF16),
            pltpu.VMEM((4, 2, 384, 128), BF16),
            pltpu.VMEM((384, 128), F32),
            pltpu.VMEM((384, 128), BF16),
            pltpu.VMEM((4, 768, 384), BF16),
            pltpu.VMEM((4, 768, 384), BF16),
            pltpu.VMEM((4, 768, 384), F32),
            pltpu.VMEM((3, 4, 2, 96, 384), BF16),
            pltpu.VMEM((3, 4, 2, 96, 384), BF16),
            pltpu.VMEM((4, 2, 96, 384), BF16),
            pltpu.SemaphoreType.DMA((SENDS,)),
            pltpu.SemaphoreType.DMA((RECVS,)),
            pltpu.SemaphoreType.DMA((4,)),
        ],
        compiler_params=pltpu.CompilerParams(
            collective_id=0, has_side_effects=True, vmem_limit_bytes=58 * 2**20
        ),
        cost_estimate=pl.CostEstimate(
            flops=6 * 10**9, bytes_accessed=4 * 10**6, transcendentals=2 * 10**5
        ),
        name="ffn_backward",
    )(tokens.T, out_grad.T, w_up, w_down)
    factor = 1.0 / math.sqrt(tokens.shape[0] * lax.axis_size("row"))
    return (ig.T, dw[:, :768].astype(F32) * factor, dw[:, 768:].astype(F32) * factor)


def solution(mesh):
    return jax.shard_map(
        body,
        mesh=mesh,
        in_specs=(P("row", "col"), P("row", "col"), P("row", "col"), P("row", "col")),
        out_specs=(P("row", "col"), P("row", "col"), P("row", "col")),
        check_vma=False,
    )
```
